128 devices in a mesh: dp: 32 (over y, z, core), mp: 4 (over x).
Axes of the slice: x: 4, y: 4, z: 4, core: 2. Of those that a mesh axis runs over, the one named last changes fastest.
Arguments:
- features_table: bfloat16 [262144, 1024], P(('dp', 'mp')), may hold values from -6 to 6
- self_features: bfloat16 [4096, 1024], P(('dp', 'mp')), may hold values from -6 to 6
- neighbour_ids: int32 [4096, 32], P(('dp', 'mp')), may hold values from 0 to 262143, as said below
- neighbour_counts: int32 [4096], P(('dp', 'mp')), may hold values from 1 to 32
- node_owner: int32 [262144], replicated, may hold values from 0 to 127, as said below
- node_row: int32 [262144], replicated, may hold values from 0 to 2047, as said below
- list_ids: int32 [4096], P(('dp', 'mp')), may hold values from 0 to 1048575, as said below
- list_owner: int32 [1048576], replicated, may hold values from 0 to 127, as said below
- list_row: int32 [1048576], replicated, may hold values from 0 to 8191, as said below
- centroids: bfloat16 [1048576, 256], P(('dp', 'mp')), may hold values from -3 to 3
- w_self: bfloat16 [1024, 2048], P(None, 'mp'), may hold values from -0.1875 to 0.1875
- w_neigh: bfloat16 [1024, 2048], P(None, 'mp'), may hold values from -0.1875 to 0.1875
- w_query: bfloat16 [2048, 1024], P('mp'), may hold values from -0.5 to 0.5
- w_out: bfloat16 [2048, 256], P('mp'), may hold values from -0.125 to 0.125
- w_context: bfloat16 [1024, 256], replicated, may hold values from -0.375 to 0.375
Outputs:
- embedding: bfloat16 [4096, 256], P(('dp', 'mp'))
- residual_codes: float32 [16384, 2, 256], P(('dp', 'mp'))
The draws below stay inside these ranges and needn't reach their ends.
Inputs may be any that keep to these rules, and one draw needn't show every extreme that they name: `neighbour_ids`: the neighbour slots of one device (its 32 new nodes, padded slots included) name nodes stored on any one device at most 16 times, and exactly 16 times for one storing device common to all devices. `node_owner`: each device stores exactly 2048 node ids. node_row numbers the ids of each device 0 to 2047, each once. `list_ids`: the 32 new nodes of one device are assigned to lists of any one owner at most 2 times, and exactly 2 times for one owner common to all devices. `list_owner`: each device owns exactly 8192 lists. list_row numbers the lists of each device 0 to 8191, each once.
All inputs are finite; a program needn't handle non-finite values.
Results may differ from the reference program's by a relative error of at most 0.0062.
Values may be sent and summed in bfloat16 or wider, within the bound.
A program may use at most 128 MiB of HBM per device.

```python
import math
import jax
import jax.numpy as jnp
from jax import lax

F = 1024
H = 2048
O = 256
NEIGH = 32
NEW_LOC = 32
NODE_DEV = 2048
LIST_DEV = 8192
SOURCES = 128
NEW = 4096
NODES = 262144
LISTS = 1048576
CAP_F = 16
CAP_L = 2
N_DP = 32
N_MP = 4


def layout_perm(key, salt, count):
    return jax.random.permutation(jax.random.fold_in(key, salt), count).astype(jnp.int32)


def bounded_owners(key, per_block, capacity, hot_owner):

    def one_block(block_key):
        first_key, second_key = jax.random.split(block_key)
        others = jax.random.permutation(first_key, SOURCES * capacity - capacity)[:per_block - capacity] + capacity
        chosen = jnp.concatenate([jnp.arange(capacity, dtype=jnp.int32), others.astype(jnp.int32)])
        owners = (chosen // capacity + hot_owner) % SOURCES
        return owners[jax.random.permutation(second_key, per_block)]
    block_keys = jax.random.split(key, SOURCES)
    return jax.vmap(one_block)(block_keys).astype(jnp.int32)


def draw_node_owner(key, part):
    perm_nodes = layout_perm(key, 101, NODES)
    return jnp.zeros((NODES,), jnp.int32).at[perm_nodes].set(jnp.arange(NODES, dtype=jnp.int32) // NODE_DEV)


def draw_node_row(key, part):
    perm_nodes = layout_perm(key, 101, NODES)
    return jnp.zeros((NODES,), jnp.int32).at[perm_nodes].set(jnp.arange(NODES, dtype=jnp.int32) % NODE_DEV)


def draw_list_owner(key, part):
    perm_lists = layout_perm(key, 201, LISTS)
    return jnp.zeros((LISTS,), jnp.int32).at[perm_lists].set(jnp.arange(LISTS, dtype=jnp.int32) // LIST_DEV)


def draw_list_row(key, part):
    perm_lists = layout_perm(key, 201, LISTS)
    return jnp.zeros((LISTS,), jnp.int32).at[perm_lists].set(jnp.arange(LISTS, dtype=jnp.int32) % LIST_DEV)


def draw_neighbour_ids(key, part):
    perm_nodes = layout_perm(key, 101, NODES)
    key = jax.random.fold_in(key, 15)
    hot_owner = jax.random.randint(jax.random.fold_in(key, 1), (), 0, SOURCES)
    owners = bounded_owners(jax.random.fold_in(key, 2), NEIGH * NEW_LOC, CAP_F, hot_owner)
    rows = jax.random.randint(jax.random.fold_in(key, 3), (SOURCES, NEIGH * NEW_LOC), 0, NODE_DEV)
    return perm_nodes[owners * NODE_DEV + rows].reshape(NEW, NEIGH).astype(jnp.int32)


def draw_list_ids(key, part):
    perm_lists = layout_perm(key, 201, LISTS)
    key = jax.random.fold_in(key, 16)
    hot_owner = jax.random.randint(jax.random.fold_in(key, 1), (), 0, SOURCES)
    owners = bounded_owners(jax.random.fold_in(key, 2), NEW_LOC, CAP_L, hot_owner)
    rows = jax.random.randint(jax.random.fold_in(key, 3), (SOURCES, NEW_LOC), 0, LIST_DEV)
    return perm_lists[owners * LIST_DEV + rows].reshape(NEW).astype(jnp.int32)


def place_ends(array, rng, smallest, high):
    longest = array.shape.index(max(array.shape))
    spots = []
    for shift in (0, 1):
        where = [jax.random.randint(jax.random.fold_in(rng, axis), (), 0, length) for axis, length in enumerate(array.shape)]
        where[longest] = (where[longest] + shift) % array.shape[longest]
        spots.append(tuple(where))
    return array.at[spots[0]].set(smallest).at[spots[1]].set(high)


def steps_of(own_key, extent, cuts, least, largest):
    level = 1.0
    for position, blocks in cuts:
        heights = jax.random.uniform(jax.random.fold_in(jax.random.fold_in(own_key, 6), position), (blocks,), jnp.float32, least / len(cuts), largest / len(cuts))
        level = level * jnp.repeat(jnp.exp(heights), extent[position] // blocks).reshape((-1,) + (1,) * (len(extent) - 1 - position))
    return level


def gaussian(rng, extent, width, reach, shards=(), held_as=jnp.bfloat16):
    loudness = steps_of(rng, extent, shards, -0.22, 0.18) if shards else 1.0
    values = jax.random.normal(rng, extent, jnp.float32) * width * loudness
    return jnp.minimum(jnp.maximum(values, -reach), reach).astype(held_as)


def setup_inputs(seed: int = 0) -> dict:
    arg_keys = jax.random.split(jax.random.key(seed), 16)
    features_table = gaussian(arg_keys[0], (NODES, F), 1.0, 6.0, ((0, 128),))
    self_features = gaussian(arg_keys[1], (NEW, F), 1.0, 6.0, ((0, 128),))
    neighbour_ids = draw_neighbour_ids(jax.random.fold_in(arg_keys[15], 71), 0)
    neighbour_counts = place_ends(jax.random.randint(arg_keys[3], (NEW,), 1, NEIGH + 1), jax.random.fold_in(arg_keys[3], 1), 1, NEIGH).astype(jnp.int32)
    node_owner = draw_node_owner(jax.random.fold_in(arg_keys[15], 71), 0)
    node_row = draw_node_row(jax.random.fold_in(arg_keys[15], 71), 0)
    list_ids = draw_list_ids(jax.random.fold_in(arg_keys[15], 71), 0)
    list_owner = draw_list_owner(jax.random.fold_in(arg_keys[15], 71), 0)
    list_row = draw_list_row(jax.random.fold_in(arg_keys[15], 71), 0)
    centroids = gaussian(arg_keys[9], (LISTS, O), 0.5, 3.0, ((0, 128),))
    w_self = gaussian(arg_keys[10], (F, H), F ** -0.5, 0.1875, ((1, 4),))
    w_neigh = gaussian(arg_keys[11], (F, H), F ** -0.5, 0.1875, ((1, 4),))
    w_query = gaussian(arg_keys[12], (H, F), (H // 16) ** -0.5, 0.5, ((0, 4),))
    w_out = gaussian(arg_keys[13], (H, O), H ** -0.5, 0.125, ((0, 4),))
    w_context = gaussian(arg_keys[14], (F, O), (F // 4) ** -0.5, 0.375)
    return dict(features_table=features_table, self_features=self_features, neighbour_ids=neighbour_ids, neighbour_counts=neighbour_counts, node_owner=node_owner, node_row=node_row, list_ids=list_ids, list_owner=list_owner, list_row=list_row, centroids=centroids, w_self=w_self, w_neigh=w_neigh, w_query=w_query, w_out=w_out, w_context=w_context)


def rms_rows(values):
    return values * lax.rsqrt(lax.optimization_barrier(jnp.mean(values * values, axis=-1, keepdims=True)) + 1e-06)

def reference(features_table, self_features, neighbour_ids, neighbour_counts, node_owner, node_row, list_ids, list_owner, list_row, centroids, w_self, w_neigh, w_query, w_out, w_context):
    sources = N_DP * N_MP
    table_index = (node_owner[neighbour_ids] * NODE_DEV + node_row[neighbour_ids]).astype(jnp.int32)
    slot_iota = lax.broadcasted_iota(jnp.int32, (NEW, NEIGH), 1)
    valid = slot_iota < neighbour_counts[:, None]
    valid_mask = valid.astype(jnp.float32)
    counts_f = neighbour_counts.astype(jnp.float32)[:, None]
    block_rows = math.gcd(NEW, 512)
    blocks = NEW // block_rows
    index_blocks = table_index.reshape(blocks, block_rows, NEIGH)
    mask_blocks = valid_mask.reshape(blocks, block_rows, NEIGH)

    def first_pass(item):
        index_block, mask_block = item
        neighbour_rows = features_table[index_block].astype(jnp.float32)
        return jnp.einsum('nj,njf->nf', mask_block, neighbour_rows)
    masked_sums = lax.map(first_pass, (index_blocks, mask_blocks)).reshape(NEW, F)
    aggregate = (masked_sums / counts_f).astype(jnp.bfloat16)
    norm_self = rms_rows(self_features.astype(jnp.float32)).astype(jnp.bfloat16)
    norm_agg = rms_rows(aggregate.astype(jnp.float32)).astype(jnp.bfloat16)
    hidden = jax.nn.relu(jnp.dot(norm_self, w_self, preferred_element_type=jnp.float32) + jnp.dot(norm_agg, w_neigh, preferred_element_type=jnp.float32)).astype(jnp.bfloat16)
    queries = jnp.dot(hidden, w_query, preferred_element_type=jnp.float32).astype(jnp.bfloat16)
    query_blocks = queries.reshape(blocks, block_rows, F)

    def second_pass(item):
        index_block, mask_block, query_block = item
        neighbour_rows = features_table[index_block].astype(jnp.float32)
        scores = jnp.einsum('nf,njf->nj', query_block.astype(jnp.float32), neighbour_rows) / math.sqrt(F)
        gates = jnp.where(mask_block > 0.5, jax.nn.sigmoid(scores), 0.0).astype(jnp.bfloat16)
        return jnp.einsum('nj,njf->nf', gates.astype(jnp.float32), neighbour_rows)
    gated_sums = lax.map(second_pass, (index_blocks, mask_blocks, query_blocks)).reshape(NEW, F)
    context = (gated_sums / counts_f).astype(jnp.bfloat16)
    pre_embed = jnp.dot(hidden, w_out, preferred_element_type=jnp.float32) + jnp.dot(context, w_context, preferred_element_type=jnp.float32)
    embedding = rms_rows(pre_embed).astype(jnp.bfloat16)
    owners = list_owner[list_ids].reshape(sources, NEW_LOC).astype(jnp.int32)
    centre_index = (owners * LIST_DEV + list_row[list_ids].reshape(sources, NEW_LOC)).astype(jnp.int32)
    same_owner = owners[:, :, None] == owners[:, None, :]
    earlier = lax.broadcasted_iota(jnp.int32, (NEW_LOC, NEW_LOC), 1) < lax.broadcasted_iota(jnp.int32, (NEW_LOC, NEW_LOC), 0)
    ranks = lax.optimization_barrier(jnp.sum(jnp.logical_and(same_owner, earlier[None]).astype(jnp.int32), axis=2)).astype(jnp.int32)
    source_ids = lax.broadcasted_iota(jnp.int32, (sources, NEW_LOC), 0)
    residual_rows = embedding.reshape(sources, NEW_LOC, O).astype(jnp.float32) - centroids[centre_index].astype(jnp.float32)
    residual_codes = jnp.zeros((sources * sources, CAP_L, O), jnp.float32).at[owners * sources + source_ids, ranks].set(residual_rows)
    return (embedding, residual_codes)
```

```python
import math

import jax
import jax.numpy as jnp
from jax import lax
from jax.experimental import pallas as pl
from jax.experimental.pallas import tpu as pltpu
from jax.sharding import PartitionSpec as P

MESH = pl.DeviceIdType.MESH
F32, BF16 = jnp.float32, jnp.bfloat16
STEP = 37


def dot(a, b):
    return jnp.dot(a, b, preferred_element_type=F32)


def dot_first(a, b):
    return lax.dot_general(a, b, (((0,), (0,)), ((), ())), preferred_element_type=F32)


def rms_rows(values):
    return values * lax.rsqrt(jnp.mean(values * values, axis=-1, keepdims=True) + 1e-06)


def iota(shape, dim):
    return lax.broadcasted_iota(jnp.int32, shape, dim)


def pick(mask, values):
    return jnp.sum(jnp.where(mask, values, 0.0), axis=1, keepdims=True)


def one_hot(mask):
    return jnp.where(mask, 1.0, 0.0).astype(BF16)


def split16(values):
    high = jnp.floor(values * (1.0 / 128.0)) * 128.0
    return high.astype(BF16), (values - high).astype(BF16)


def offset(i):
    k = lax.rem(i * STEP, 128)
    return lax.rem(k, 4), lax.rem(lax.div(k, 4), 2), lax.rem(lax.div(k, 8), 4), lax.div(k, 32)


def kernel(
    ids, cnt, lids_s, lids, self_f, node_owner, node_row, list_owner, list_row, features, centroids,
    w_self, w_neigh, w_query, w_out, w_context,
    emb_out, res_out,
    no_v, nr_v, lo_v, lr_v, ft, ct, ws, wn, wq, wo, wc,
    btab, rq, ra, rbs, rb, rhi, rlo, lo_rows, lr_rows, sb, gb, plb, obt, ns, na, s1, ps, pr, cen, obuf, ea, ebs, eb,
    load_sem, send_sem, recv_sem, row_sem,
):
    dp, x = lax.axis_index("dp"), lax.axis_index("mp")
    c, yz = lax.rem(dp, 2), lax.div(dp, 2)
    z, y = lax.rem(yz, 4), lax.div(yz, 4)
    cx = c * 4 + x

    loads = [
        pltpu.make_async_copy(src, dst, load_sem.at[i])
        for i, (src, dst) in enumerate(
            [(node_owner, no_v), (node_row, nr_v), (list_owner, lo_v), (list_row, lr_v), (features, ft), (w_self, ws),
             (centroids, ct), (w_neigh, wn), (w_query, wq), (w_out, wo), (w_context, wc)]
        )
    ]
    for load in loads:
        load.start()

    barrier = pltpu.get_barrier_semaphore()

    def yz_peer(i):
        return lax.rem(yz + i, 16)

    def cx_peer(i):
        return lax.rem(cx + i, 8)

    def greet_yz(i, _):
        pl.semaphore_signal(barrier, inc=1, device_id=(yz_peer(i) * 2 + c, x), device_id_type=MESH)
        return 0

    def greet_cx(i, _):
        p = cx_peer(i)
        pl.semaphore_signal(barrier, inc=1, device_id=(yz * 2 + lax.div(p, 4), lax.rem(p, 4)), device_id_type=MESH)
        return 0

    lax.fori_loop(1, 16, greet_yz, 0)
    lax.fori_loop(1, 8, greet_cx, 0)

    def remote(src, dst, which, device, recv=None):
        return pltpu.make_async_remote_copy(
            src_ref=src, dst_ref=dst, send_sem=send_sem.at[which], recv_sem=recv_sem.at[which] if recv is None else recv,
            device_id=device, device_id_type=MESH,
        )

    def landed(ref, sem):
        pltpu.make_async_copy(ref, ref, sem).wait()

    ns[pl.ds(0, 32), :] = rms_rows(self_f[...].astype(F32)).astype(BF16)

    loads[0].wait()
    loads[1].wait()
    btab[:, 0:128] = no_v[...].astype(F32).astype(BF16)
    rows_f = nr_v[...]
    btab[:, 128:256] = lax.shift_left(lax.shift_right_logical(rows_f, 4), 4).astype(F32).astype(BF16)
    btab[:, 256:384] = jnp.bitwise_and(rows_f, 15).astype(F32).astype(BF16)
    ids_all = ids[...]
    lane = iota((256, 128), 1)
    tri = one_hot(iota((256, 256), 1) < iota((256, 256), 0))
    carry = jnp.zeros((1, 128), F32)
    slot_row = iota((256, 1), 0)
    node = (lax.rem(slot_row, 32) + 1).astype(F32)
    counts8 = jnp.concatenate([cnt[...]] * 8, axis=0)
    request = jnp.zeros((128, 128), F32)
    for q in range(4):
        idc = jnp.concatenate([ids_all[:, 8 * q + j : 8 * q + j + 1] for j in range(8)], axis=0)
        found = dot(one_hot(iota((256, 2048), 1) == lax.shift_right_logical(idc, 7)), btab[...])
        sel = lane == jnp.bitwise_and(idc, 127)
        owner = pick(sel, found[:, 0:128])
        high, low = pick(sel, found[:, 128:256]), pick(sel, found[:, 256:384])
        mine = lane.astype(F32) == owner
        hot = one_hot(mine)
        rank = pick(mine, dot(tri, hot) + carry)
        carry = carry + jnp.sum(jnp.where(mine, 1.0, 0.0), axis=0, keepdims=True)
        valid = (lax.div(slot_row, 32) + 8 * q) < counts8
        here = lane.astype(F32) == rank
        there = (lane - 32).astype(F32) == rank
        x_high = jnp.where(here, high, jnp.where(there, jnp.where(valid, node, 0.0), 0.0)).astype(BF16)
        x_low = jnp.where(here, low, 0.0).astype(BF16)
        request = request + dot_first(hot, x_high) + dot_first(hot, x_low)

    loads[2].wait()
    loads[3].wait()

    def list_lookup(n, _):
        r = lax.div(lids_s[n], 128)
        lo_rows[pl.ds(n, 1), :] = lo_v[pl.ds(r, 1), :]
        lr_rows[pl.ds(n, 1), :] = lr_v[pl.ds(r, 1), :]
        return 0

    lax.fori_loop(0, 32, list_lookup, 0, unroll=8)
    lane32 = iota((32, 128), 1)
    lsel = lane32 == jnp.bitwise_and(lids[...], 127)
    dest = pick(lsel, lo_rows[...].astype(F32))
    lrow = pick(lsel, lr_rows[...].astype(F32)) + 1.0
    lmine = lane32.astype(F32) == dest
    lhot = one_hot(lmine)
    lrank = pick(lmine, dot(one_hot(iota((32, 32), 1) < iota((32, 32), 0)), lhot))
    lhigh, llow = split16(lrow)
    lthere = (lane32 - 16).astype(F32) == lrank
    request = request + dot_first(lhot, jnp.where(lthere, lhigh.astype(F32), 0.0).astype(BF16))
    request = request + dot_first(lhot, jnp.where(lthere, llow.astype(F32), 0.0).astype(BF16))
    obt[...] = one_hot(iota((32, 256), 1).astype(F32) == dest * 2.0 + lrank)
    rq[...] = request

    pl.semaphore_wait(barrier, 22)

    def ask_yz(i, _):
        p = yz_peer(i)
        remote(rq.at[pl.ds(pl.multiple_of(p * 8, 8), 8), :], ra.at[pl.ds(pl.multiple_of(yz * 8, 8), 8), :], 0, (p * 2 + c, x)).start()
        return 0

    lax.fori_loop(1, 16, ask_yz, 0)
    own = pl.ds(pl.multiple_of(yz * 8, 8), 8)
    ra[own, :] = rq[own, :]
    landed(ra.at[pl.ds(0, 120), :], recv_sem.at[0])
    for p in range(8):
        rbs[pl.ds(16 * p, 16), :] = ra[pl.ds(p, 16, stride=8), :]

    def ask_cx(i, _):
        p = cx_peer(i)
        remote(rbs.at[pl.ds(pl.multiple_of(p * 16, 16), 16), :], rb.at[pl.ds(pl.multiple_of(cx * 16, 16), 16), :], 1, (yz * 2 + lax.div(p, 4), lax.rem(p, 4))).start()
        return 0

    lax.fori_loop(1, 8, ask_cx, 0)
    own = pl.ds(pl.multiple_of(cx * 16, 16), 16)
    rb[own, :] = rbs[own, :]

    for i in range(1, 4):
        remote(ns.at[pl.ds(0, 32), :], ns.at[pl.ds(32 * i, 32), :], 2, (dp, lax.rem(x + i, 4))).start()

    order_row, order_lane = iota((128, 128), 0), iota((128, 128), 1)
    kx, kc, kz, ky = offset(order_row)
    from_owner = (lax.rem(y + 4 - ky, 4) * 4 + lax.rem(z + 4 - kz, 4)) * 8 + lax.rem(c + kc, 2) * 4 + lax.rem(x + 4 - kx, 4)
    to_asker = (lax.rem(c + kc, 2) * 4 + lax.rem(x + kx, 4)) * 16 + lax.rem(y + ky, 4) * 4 + lax.rem(z + kz, 4)
    spread = one_hot(lax.div(iota((256, 16), 0), 16) == iota((256, 16), 1))
    sub = lax.rem(iota((256, 128), 0), 16)
    nodes = dot(one_hot(order_lane == from_owner), split16(request)[1]).astype(BF16)
    for g in range(8):
        held = pick(lane == sub + 32, dot(spread, nodes[16 * g : 16 * g + 16, :]))
        member = jnp.where((lane + 1).astype(F32) == held, 1.0, 0.0)
        plb[:, 256 * g : 256 * g + 256] = jnp.transpose(member)[0:32, :].astype(BF16)

    loads[4].wait()
    landed(rb.at[pl.ds(0, 112), :], recv_sem.at[1])

    asker = one_hot(order_lane == to_asker)
    asked_high, asked_low = split16(rb[...])
    rhi[...] = dot(asker, asked_high)
    rlo[...] = dot(asker, asked_low)

    def serve(g, _):
        block = pl.ds(pl.multiple_of(16 * g, 16), 16)
        asked = dot(spread, rhi[block, :].astype(BF16)) + dot(spread, rlo[block, :].astype(BF16))
        index = pick(lane == sub, asked).astype(jnp.int32)
        rows = dot(one_hot(iota((256, 2048), 1) == index), ft[...]).astype(BF16)
        sb[pl.ds(pl.multiple_of(256 * g, 256), 256), :] = rows

        def send(j, _):
            i = 16 * g + j
            kx, kc, kz, ky = offset(i)
            device = ((lax.rem(y + ky, 4) * 4 + lax.rem(z + kz, 4)) * 2 + lax.rem(c + kc, 2), lax.rem(x + kx, 4))
            part = pl.ds(pl.multiple_of(16 * i, 16), 16)
            remote(sb.at[part, :], gb.at[part, :], 3, device, row_sem.at[g]).start()
            return 0

        lax.fori_loop(jnp.where(g == 0, 1, 0), 16, send, 0)
        return 0

    lax.fori_loop(0, 8, serve, 0)
    gb[pl.ds(0, 16), :] = sb[pl.ds(0, 16), :]

    landed(ns.at[pl.ds(32, 96), :], recv_sem.at[2])
    loads[5].wait()
    s1[...] = dot(ns[...], ws[...])
    loads[6].wait()
    lists = jnp.concatenate([rb[pl.ds(p, 8, stride=16), :] for p in range(16)], axis=0)
    wanted = jnp.concatenate([lists[:, 16:17], lists[:, 17:18]], axis=0)
    wanted_i = wanted.astype(jnp.int32) - 1

    def centre(k, total):
        hot = one_hot(iota((256, 1024), 1) + 1024 * k == wanted_i)
        return total + dot(hot, ct[pl.ds(pl.multiple_of(1024 * k, 1024), 1024), :])

    cen[...] = lax.fori_loop(0, 8, centre, jnp.zeros((256, 256), F32))

    total = jnp.zeros((32, 1024), F32)
    for g in range(8):
        first = 16 if g == 0 else 0
        landed(gb.at[pl.ds(256 * g + first, 256 - first), :], row_sem.at[g])
        total = total + dot(plb[:, 256 * g : 256 * g + 256], gb[pl.ds(256 * g, 256), :])
    counts = cnt[...].astype(F32)
    aggregate = (total / counts).astype(BF16)
    na[pl.ds(0, 32), :] = rms_rows(aggregate.astype(F32)).astype(BF16)
    for i in range(1, 4):
        remote(na.at[pl.ds(0, 32), :], na.at[pl.ds(32 * i, 32), :], 4, (dp, lax.rem(x + i, 4))).start()
    for load in loads[7:]:
        load.wait()
    landed(na.at[pl.ds(32, 96), :], recv_sem.at[4])
    hidden = jnp.maximum(s1[...] + dot(na[...], wn[...]), 0.0).astype(BF16)
    ps[:, 0:1024] = dot(hidden, wq[...])
    ps[:, 1024:1280] = dot(hidden, wo[...])
    for i in range(1, 4):
        part = pl.ds(32 * i, 32)
        remote(ps.at[part, :], pr.at[part, :], 5, (dp, lax.rem(x + 4 - i, 4))).start()
    pr[pl.ds(0, 32), :] = ps[pl.ds(0, 32), :]
    landed(pr.at[pl.ds(32, 96), :], recv_sem.at[5])
    terms = (pr[pl.ds(0, 32), :] + pr[pl.ds(32, 32), :]) + (pr[pl.ds(64, 32), :] + pr[pl.ds(96, 32), :])
    queries = terms[:, 0:1024].astype(BF16)
    scores = lax.dot_general(queries, gb[...], (((1,), (1,)), ((), ())), preferred_element_type=F32)
    gates = jnp.where(plb[...].astype(F32) > 0.5, jax.nn.sigmoid(scores * (1.0 / 32.0)), 0.0).astype(BF16)
    context = (dot(gates, gb[...]) / counts).astype(BF16)
    embedding = rms_rows(terms[:, 1024:1280] + dot(context, wc[...])).astype(BF16)
    emb_out[...] = embedding

    obuf[...] = dot_first(obt[...], embedding).astype(BF16)

    def tell_yz(i, _):
        p = yz_peer(i)
        remote(obuf.at[pl.ds(pl.multiple_of(p * 16, 16), 16), :], ea.at[pl.ds(pl.multiple_of(yz * 16, 16), 16), :], 6, (p * 2 + c, x)).start()
        return 0

    lax.fori_loop(1, 16, tell_yz, 0)
    own = pl.ds(pl.multiple_of(yz * 16, 16), 16)
    ea[own, :] = obuf[own, :]
    r0, r1 = iota((256, 256), 0), iota((256, 256), 1)
    turn = one_hot(r1 == lax.rem(r0, 16) * 16 + lax.div(r0, 32) * 2 + lax.rem(lax.div(r0, 16), 2))
    back = one_hot(r1 == lax.rem(r0, 8) * 32 + lax.div(r0, 128) * 16 + lax.rem(lax.div(r0, 8), 16))
    landed(ea.at[pl.ds(0, 240), :], recv_sem.at[6])
    ebs[...] = dot(turn, ea[...]).astype(BF16)

    def tell_cx(i, _):
        p = cx_peer(i)
        remote(ebs.at[pl.ds(pl.multiple_of(p * 32, 32), 32), :], eb.at[pl.ds(pl.multiple_of(cx * 32, 32), 32), :], 7, (yz * 2 + lax.div(p, 4), lax.rem(p, 4))).start()
        return 0

    lax.fori_loop(1, 8, tell_cx, 0)
    own = pl.ds(pl.multiple_of(cx * 32, 32), 32)
    eb[own, :] = ebs[own, :]
    landed(eb.at[pl.ds(0, 224), :], recv_sem.at[7])
    arrived = dot(back, eb[...])
    res_out[...] = jnp.where(wanted > 0.5, arrived - cen[...], 0.0)

    landed(rq.at[pl.ds(0, 120), :], send_sem.at[0])
    landed(rbs.at[pl.ds(0, 112), :], send_sem.at[1])
    landed(ns.at[pl.ds(0, 96), :], send_sem.at[2])
    landed(sb.at[pl.ds(16, 2032), :], send_sem.at[3])
    landed(na.at[pl.ds(0, 96), :], send_sem.at[4])
    landed(ps.at[pl.ds(32, 96), :], send_sem.at[5])
    landed(obuf.at[pl.ds(0, 240), :], send_sem.at[6])
    landed(ebs.at[pl.ds(0, 224), :], send_sem.at[7])


def local(
    features_table, self_features, neighbour_ids, neighbour_counts, node_owner, node_row, list_ids, list_owner,
    list_row, centroids, w_self, w_neigh, w_query, w_out, w_context,
):
    vmem, smem, anyw = (pl.BlockSpec(memory_space=m) for m in (pltpu.VMEM, pltpu.SMEM, pl.ANY))
    i32 = jnp.int32
    scratch = [
        ((2048, 128), i32), ((2048, 128), i32), ((8192, 128), i32), ((8192, 128), i32), ((2048, 1024), BF16),
        ((8192, 256), BF16), ((1024, 512), BF16), ((1024, 512), BF16), ((512, 1024), BF16), ((512, 256), BF16),
        ((1024, 256), BF16),
        ((2048, 384), BF16), ((128, 128), F32), ((128, 128), F32), ((128, 128), F32), ((128, 128), F32),
        ((128, 128), F32), ((128, 128), F32), ((32, 128), i32), ((32, 128), i32),
        ((2048, 1024), BF16), ((2048, 1024), BF16), ((32, 2048), BF16), ((32, 256), BF16), ((128, 1024), BF16),
        ((128, 1024), BF16), ((128, 512), F32), ((128, 1280), F32), ((128, 1280), F32), ((256, 256), F32),
        ((256, 256), BF16), ((256, 256), BF16), ((256, 256), BF16), ((256, 256), BF16),
    ]
    embedding, residual = pl.pallas_call(
        kernel,
        out_shape=(jax.ShapeDtypeStruct((32, 256), BF16), jax.ShapeDtypeStruct((256, 256), F32)),
        in_specs=[vmem, vmem, smem, vmem, vmem] + [anyw] * 11,
        out_specs=(vmem, vmem),
        scratch_shapes=[pltpu.VMEM(s, t) for s, t in scratch]
        + [pltpu.SemaphoreType.DMA((11,)), pltpu.SemaphoreType.DMA((8,)), pltpu.SemaphoreType.DMA((8,)), pltpu.SemaphoreType.DMA((8,))],
        compiler_params=pltpu.CompilerParams(collective_id=0, has_side_effects=True, vmem_limit_bytes=56 << 20),
    )(
        neighbour_ids, neighbour_counts.reshape(32, 1), list_ids, list_ids.reshape(32, 1), self_features,
        node_owner.reshape(2048, 128), node_row.reshape(2048, 128), list_owner.reshape(8192, 128),
        list_row.reshape(8192, 128), features_table, centroids, w_self, w_neigh, w_query, w_out, w_context,
    )
    return embedding, residual.reshape(2, 128, 256).transpose(1, 0, 2)


def solution(mesh):
    placed = (
        P(("dp", "mp"), None),
        P(("dp", "mp"), None),
        P(("dp", "mp"), None),
        P(("dp", "mp")),
        P(),
        P(),
        P(("dp", "mp")),
        P(),
        P(),
        P(("dp", "mp"), None),
        P(None, "mp"),
        P(None, "mp"),
        P("mp", None),
        P("mp", None),
        P(),
    )
    return jax.shard_map(
        local,
        mesh=mesh,
        in_specs=placed,
        out_specs=(P(("dp", "mp"), None), P(("dp", "mp"), None, None)),
        check_vma=False,
    )
```

```python
import math

import jax
import jax.numpy as jnp
from jax import lax
from jax.experimental import pallas as pl
from jax.experimental.pallas import tpu as pltpu
from jax.sharding import PartitionSpec as P

MESH = pl.DeviceIdType.MESH
F32, BF16 = jnp.float32, jnp.bfloat16


def dot(a, b):
    return jnp.dot(a, b, preferred_element_type=F32)


def dot_first(a, b):
    return lax.dot_general(a, b, (((0,), (0,)), ((), ())), preferred_element_type=F32)


def rms_rows(values):
    return values * lax.rsqrt(jnp.mean(values * values, axis=-1, keepdims=True) + 1e-06)


def iota(shape, dim):
    return lax.broadcasted_iota(jnp.int32, shape, dim)


def pick(mask, values):
    return jnp.sum(jnp.where(mask, values, 0.0), axis=1, keepdims=True)


def spread_pick(mask, values, ones):
    return dot(jnp.where(mask, values, 0.0).astype(BF16), ones)


def column(row):
    return jnp.sum(jnp.where(iota((32, 32), 0) == iota((32, 32), 1), row.astype(F32), 0.0), axis=1, keepdims=True)


def one_hot(mask):
    return jnp.where(mask, 1.0, 0.0).astype(BF16)


def split16(values):
    high = jnp.floor(values * (1.0 / 128.0)) * 128.0
    return high.astype(BF16), (values - high).astype(BF16)


def offset(i):
    g, a, b = lax.div(i, 16), lax.div(lax.rem(i, 16), 4), lax.rem(i, 4)
    return b, lax.rem(lax.div(g, 4) + a + lax.div(b, 2), 2), lax.rem(a + b, 4), lax.rem(g + a + 3 * b, 4)


def kernel(
    ids, cnt, lids_s, lids, self_f, node_owner, node_row, list_owner, list_row, features, centroids,
    w_self, w_neigh, w_query, w_out, w_context,
    emb_out, eb, cen,
    no_v, nr_v, lo_v, lr_v, ft, ct, ws, wn, wq, wo, wc,
    btab, rq, rb, held, lo_rows, lr_rows, sb, gb, plb, obt, ns, na, s1, ps, pr, ob, load_sem, send_sem, recv_sem, ask_sem, row_sem,
):
    dp, x = lax.axis_index("dp"), lax.axis_index("mp")
    c, yz = lax.rem(dp, 2), lax.div(dp, 2)
    z, y = lax.rem(yz, 4), lax.div(yz, 4)
    me = dp * 4 + x

    def partners(g, sign):
        xs = [lax.rem(x + (sign * k) % 4, 4) for k in range(4)]
        zs = [lax.rem(z + (sign * k) % 4, 4) * 2 for k in range(4)]
        ys = [lax.rem(y + 16 + sign * (g + k), 4) * 8 for k in range(4)]
        cs = [lax.rem(c + lax.div(g, 4) + k, 2) for k in range(2)]
        return [
            (ys[(j // 4 + 3 * (j % 4)) % 4] + zs[(j // 4 + j % 4) % 4] + cs[(j // 4 + j % 4 // 2) % 2], xs[j % 4])
            for j in range(16)
        ]

    loads = [
        pltpu.make_async_copy(src, dst, load_sem.at[i])
        for i, (src, dst) in enumerate(
            [(node_owner, no_v), (node_row, nr_v), (list_owner, lo_v), (list_row, lr_v), (features, ft), (w_self, ws),
             (centroids, ct), (w_neigh, wn), (w_query, wq), (w_out, wo), (w_context, wc)]
        )
    ]
    for load in loads:
        load.start()

    barrier = pltpu.get_barrier_semaphore()

    def greet(j_first):
        def body(g, _):
            for device in partners(g, 1)[j_first:]:
                pl.semaphore_signal(barrier, inc=1, device_id=device, device_id_type=MESH)
            return 0

        return body

    greet(1)(jnp.int32(0), 0)
    lax.fori_loop(1, 8, greet(0), 0)

    def remote(src, dst, which, device, recv=None):
        return pltpu.make_async_remote_copy(
            src_ref=src, dst_ref=dst, send_sem=send_sem.at[which], recv_sem=recv_sem.at[which] if recv is None else recv,
            device_id=device, device_id_type=MESH,
        )

    def landed(ref, sem):
        pltpu.make_async_copy(ref, ref, sem).wait()

    ns[pl.ds(0, 32), :] = rms_rows(self_f[...].astype(F32)).astype(BF16)

    loads[0].wait()
    loads[1].wait()
    code = no_v[...] * 2048 + nr_v[...]
    btab[:, 0:128] = (lax.shift_right_logical(code, 9) - 256).astype(F32).astype(BF16)
    btab[:, 128:256] = (jnp.bitwise_and(code, 511) - 256).astype(F32).astype(BF16)
    ones = jnp.ones((128, 128), BF16)
    counts = column(cnt[...])
    ids_all = ids[...]
    lane = iota((256, 128), 1)
    lane_f = lane.astype(F32)
    tri = one_hot(iota((256, 256), 1) < iota((256, 256), 0))
    carry = jnp.zeros((1, 128), F32)
    slot_row = iota((256, 1), 0)
    node = (lax.rem(slot_row, 32) + 1).astype(F32)
    counts8 = jnp.concatenate([counts] * 8, axis=0)
    request = jnp.zeros((128, 128), F32)
    for q in range(4):
        idc = jnp.concatenate([ids_all[:, 8 * q + j : 8 * q + j + 1] for j in range(8)], axis=0)
        found = dot(one_hot(iota((256, 2048), 1) == lax.shift_right_logical(idc, 7)), btab[...])
        sel = lane == jnp.bitwise_and(idc, 127)
        code = (spread_pick(sel, found[:, 0:128], ones) + 256.0) * 512.0 + (spread_pick(sel, found[:, 128:256], ones) + 256.0)
        owner = jnp.floor(code * (1.0 / 2048.0))
        row = code - owner * 2048.0
        high = jnp.floor(row * (1.0 / 16.0)) * 16.0
        low = row - high
        mine = lane_f == owner
        hot = one_hot(mine)
        rank = spread_pick(mine, dot(tri, hot) + carry, ones)
        carry = carry + jnp.sum(jnp.where(mine, 1.0, 0.0), axis=0, keepdims=True)
        valid = (lax.div(slot_row, 32) + 8 * q).astype(F32) < counts8
        here = lane_f == rank
        there = lane_f - 32.0 == rank
        x_high = jnp.where(here, high, jnp.where(there, jnp.where(valid, node, 0.0), 0.0)).astype(BF16)
        x_low = jnp.where(here, low, 0.0).astype(BF16)
        request = request + dot_first(hot, x_high) + dot_first(hot, x_low)

    loads[2].wait()
    loads[3].wait()

    def list_lookup(n, _):
        r = lax.div(lids_s[n], 128)
        lo_rows[pl.ds(n, 1), :] = lo_v[pl.ds(r, 1), :]
        lr_rows[pl.ds(n, 1), :] = lr_v[pl.ds(r, 1), :]
        return 0

    lax.fori_loop(0, 32, list_lookup, 0, unroll=8)
    lane32 = iota((32, 128), 1)
    lsel = lane32 == column(jnp.bitwise_and(lids[...], 127)).astype(jnp.int32)
    dest = pick(lsel, lo_rows[...].astype(F32))
    lrow = pick(lsel, lr_rows[...].astype(F32)) + 1.0
    lmine = lane32.astype(F32) == dest
    lhot = one_hot(lmine)
    lrank = pick(lmine, dot(one_hot(iota((32, 32), 1) < iota((32, 32), 0)), lhot))
    lhigh, llow = split16(lrow)
    lthere = (lane32 - 16).astype(F32) == lrank
    request = request + dot_first(lhot, jnp.where(lthere, lhigh.astype(F32), 0.0).astype(BF16))
    request = request + dot_first(lhot, jnp.where(lthere, llow.astype(F32), 0.0).astype(BF16))
    obt[...] = one_hot(iota((32, 256), 1).astype(F32) == dest + 128.0 * lrank)

    order_row, order_lane = iota((128, 128), 0), iota((128, 128), 1)
    kx, kc, kz, ky = offset(order_row)
    from_dp = (lax.rem(y + 4 - ky, 4) * 4 + lax.rem(z + 4 - kz, 4)) * 2 + lax.rem(c + kc, 2)
    asked = one_hot(order_lane == from_dp * 4 + lax.rem(x + 4 - kx, 4))
    high, low = split16(request)
    low = dot(asked, low)
    held[...] = low.astype(BF16)
    rq[:, 0, :] = dot(asked, high) + low

    pl.semaphore_wait(barrier, 127)

    def ask(j_first):
        def body(g, _):
            for j, device in list(enumerate(partners(g, -1)))[j_first:]:
                i = 16 * g + j
                remote(rq.at[i], rb.at[i], 0, device, ask_sem.at[g]).start()
            return 0

        return body

    pltpu.make_async_copy(rq.at[0], rb.at[0], ask_sem.at[0]).start()
    ask(1)(0, 0)
    lax.fori_loop(1, 8, ask(0), 0)

    for i in range(1, 4):
        remote(ns.at[pl.ds(0, 32), :], ns.at[pl.ds(32 * i, 32), :], 2, (dp, lax.rem(x + i, 4))).start()

    spread = one_hot(lax.div(iota((256, 16), 0), 16) == iota((256, 16), 1))
    sub = lax.rem(iota((256, 128), 0), 16)
    loads[4].wait()

    def serve(j_first):
        def body(g, _):
            block = pl.ds(pl.multiple_of(16 * g, 16), 16)
            landed(rb.at[block], ask_sem.at[g])
            high, low = split16(rb[block, 0, :])
            index = pick(lane == sub, dot(spread, high) + dot(spread, low)).astype(jnp.int32)
            rows = dot(one_hot(iota((256, 2048), 1) == index), ft[...]).astype(BF16)
            sb[pl.ds(pl.multiple_of(256 * g, 256), 256), :] = rows
            for j, device in list(enumerate(partners(g, 1)))[j_first:]:
                part = pl.ds(pl.multiple_of(256 * g + 16 * j, 16), 16)
                remote(sb.at[part, :], gb.at[part, :], 3, device, row_sem.at[g]).start()
            return 0

        return body

    serve(1)(0, 0)
    own_rows = pltpu.make_async_copy(sb.at[pl.ds(0, 16), :], gb.at[pl.ds(0, 16), :], row_sem.at[0])
    own_rows.start()
    lax.fori_loop(1, 8, serve(0), 0)

    for g in range(8):
        node = pick(lane == sub + 32, dot(spread, held[pl.ds(16 * g, 16), :]))
        member = jnp.where(lane_f + 1.0 == node, 1.0, 0.0)
        plb[:, 256 * g : 256 * g + 256] = jnp.transpose(member)[0:32, :].astype(BF16)


    landed(ns.at[pl.ds(32, 96), :], recv_sem.at[2])
    loads[5].wait()
    s1[...] = dot(ns[...], ws[...])
    loads[6].wait()
    kx, kc, kz, ky = offset(order_lane)
    to_dp = (lax.rem(y + ky, 4) * 4 + lax.rem(z + kz, 4)) * 2 + lax.rem(c + kc, 2)
    by_source = one_hot(order_row == to_dp * 4 + lax.rem(x + kx, 4))
    high, low = split16(rb[:, 0, :])
    lists = dot(by_source, high) + dot(by_source, low)
    wanted = jnp.concatenate([lists[:, 16:17], lists[:, 17:18]], axis=0).astype(jnp.int32) - 1

    def centre(k, total):
        hot = one_hot(iota((256, 1024), 1) + 1024 * k == wanted)
        return total + dot(hot, ct[pl.ds(pl.multiple_of(1024 * k, 1024), 1024), :])

    centres = lax.fori_loop(0, 8, centre, jnp.zeros((256, 256), F32))
    cen[:, 0, :] = centres[0:128, :]
    cen[:, 1, :] = centres[128:256, :]

    total = jnp.zeros((32, 1024), F32)
    for g in range(8):
        landed(gb.at[pl.ds(256 * g, 256), :], row_sem.at[g])
        total = total + dot(plb[:, 256 * g : 256 * g + 256], gb[pl.ds(256 * g, 256), :])
    aggregate = (total / counts).astype(BF16)
    na[pl.ds(0, 32), :] = rms_rows(aggregate.astype(F32)).astype(BF16)
    for i in range(1, 4):
        remote(na.at[pl.ds(0, 32), :], na.at[pl.ds(32 * i, 32), :], 4, (dp, lax.rem(x + i, 4))).start()
    for load in loads[7:]:
        load.wait()
    landed(na.at[pl.ds(32, 96), :], recv_sem.at[4])
    hidden = jnp.maximum(s1[...] + dot(na[...], wn[...]), 0.0).astype(BF16)
    to_query, to_head = dot(hidden, wq[...]), dot(hidden, wo[...])
    ps[:, 0:1024] = to_query.astype(BF16)
    ps[:, 1024:1280] = to_head.astype(BF16)
    for i in range(1, 4):
        part = pl.ds(32 * i, 32)
        remote(ps.at[part, :], pr.at[part, :], 5, (dp, lax.rem(x + 4 - i, 4))).start()
    landed(pr.at[pl.ds(32, 96), :], recv_sem.at[5])
    others = (pr[pl.ds(32, 32), :].astype(F32) + pr[pl.ds(64, 32), :].astype(F32)) + pr[pl.ds(96, 32), :].astype(F32)
    terms = jnp.concatenate([to_query[0:32, :], to_head[0:32, :]], axis=1) + others
    queries = terms[:, 0:1024].astype(BF16)
    scores = lax.dot_general(queries, gb[...], (((1,), (1,)), ((), ())), preferred_element_type=F32)
    gates = jnp.where(plb[...].astype(F32) > 0.5, jax.nn.sigmoid(scores * (1.0 / 32.0)), 0.0).astype(BF16)
    context = (dot(gates, gb[...]) / counts).astype(BF16)
    embedding = rms_rows(terms[:, 1024:1280] + dot(context, wc[...])).astype(BF16)
    emb_out[...] = embedding

    slots = dot_first(obt[...], embedding)
    ob[:, 0, :] = slots[0:128, :]
    ob[:, 1, :] = slots[128:256, :]

    def tell(j_first):
        def body(g, _):
            for dp_to, x_to in partners(g, 1)[j_first:]:
                remote(ob.at[dp_to * 4 + x_to], eb.at[me], 6, (dp_to, x_to)).start()
            return 0

        return body

    tell(1)(0, 0)
    lax.fori_loop(1, 8, tell(0), 0)
    own_slots = pltpu.make_async_copy(ob.at[me], eb.at[me], recv_sem.at[6])
    own_slots.start()
    landed(eb, recv_sem.at[6])

    landed(rq.at[pl.ds(0, 127)], send_sem.at[0])
    landed(ns.at[pl.ds(0, 96), :], send_sem.at[2])
    landed(sb.at[pl.ds(16, 2032), :], send_sem.at[3])
    landed(na.at[pl.ds(0, 96), :], send_sem.at[4])
    landed(ps.at[pl.ds(32, 96), :], send_sem.at[5])
    landed(ob.at[pl.ds(0, 127)], send_sem.at[6])


def local(
    features_table, self_features, neighbour_ids, neighbour_counts, node_owner, node_row, list_ids, list_owner,
    list_row, centroids, w_self, w_neigh, w_query, w_out, w_context,
):
    vmem, smem, anyw = (pl.BlockSpec(memory_space=m) for m in (pltpu.VMEM, pltpu.SMEM, pl.ANY))
    i32 = jnp.int32
    scratch = [
        ((2048, 128), i32), ((2048, 128), i32), ((8192, 128), i32), ((8192, 128), i32), ((2048, 1024), BF16),
        ((8192, 256), BF16), ((1024, 512), BF16), ((1024, 512), BF16), ((512, 1024), BF16), ((512, 256), BF16),
        ((1024, 256), BF16),
        ((2048, 256), BF16), ((128, 1, 128), F32), ((128, 1, 128), F32), ((128, 128), BF16), ((32, 128), i32), ((32, 128), i32),
        ((2048, 1024), BF16), ((2048, 1024), BF16), ((32, 2048), BF16), ((32, 256), BF16), ((128, 1024), BF16),
        ((128, 1024), BF16), ((128, 512), F32), ((128, 1280), BF16), ((128, 1280), BF16), ((128, 2, 256), F32),
    ]
    embedding, arrived, centres = pl.pallas_call(
        kernel,
        out_shape=(jax.ShapeDtypeStruct((32, 256), BF16),) + (jax.ShapeDtypeStruct((128, 2, 256), F32),) * 2,
        in_specs=[vmem, vmem, smem, vmem, vmem] + [anyw] * 11,
        out_specs=(vmem, vmem, vmem),
        scratch_shapes=[pltpu.VMEM(s, t) for s, t in scratch]
        + [pltpu.SemaphoreType.DMA((n,)) for n in (11, 8, 8, 8, 8)],
        compiler_params=pltpu.CompilerParams(collective_id=0, has_side_effects=True, vmem_limit_bytes=56 << 20),
    )(
        neighbour_ids, neighbour_counts.reshape(1, 32), list_ids, list_ids.reshape(1, 32), self_features,
        node_owner.reshape(2048, 128), node_row.reshape(2048, 128), list_owner.reshape(8192, 128),
        list_row.reshape(8192, 128), features_table, centroids, w_self, w_neigh, w_query, w_out, w_context,
    )
    return embedding, arrived - centres


def solution(mesh):
    placed = (
        P(("dp", "mp"), None),
        P(("dp", "mp"), None),
        P(("dp", "mp"), None),
        P(("dp", "mp")),
        P(),
        P(),
        P(("dp", "mp")),
        P(),
        P(),
        P(("dp", "mp"), None),
        P(None, "mp"),
        P(None, "mp"),
        P("mp", None),
        P("mp", None),
        P(),
    )
    return jax.shard_map(
        local,
        mesh=mesh,
        in_specs=placed,
        out_specs=(P(("dp", "mp"), None), P(("dp", "mp"), None, None)),
        check_vma=False,
    )
```

```python
import math

import jax
import jax.numpy as jnp
from jax import lax
from jax.experimental import pallas as pl
from jax.experimental.pallas import tpu as pltpu
from jax.sharding import PartitionSpec as P

MESH = pl.DeviceIdType.MESH
F32, BF16 = jnp.float32, jnp.bfloat16


def dot(a, b):
    return jnp.dot(a, b, preferred_element_type=F32)


def dot_first(a, b):
    return lax.dot_general(a, b, (((0,), (0,)), ((), ())), preferred_element_type=F32)


def rms_rows(values):
    return values * lax.rsqrt(jnp.mean(values * values, axis=-1, keepdims=True) + 1e-06)


def iota(shape, dim):
    return lax.broadcasted_iota(jnp.int32, shape, dim)


def pick(mask, values):
    return jnp.sum(jnp.where(mask, values, 0.0), axis=1, keepdims=True)


def spread_pick(mask, values, ones):
    return dot(jnp.where(mask, values, 0.0).astype(BF16), ones)


def column(row):
    return jnp.sum(jnp.where(iota((32, 32), 0) == iota((32, 32), 1), row.astype(F32), 0.0), axis=1, keepdims=True)


def one_hot(mask):
    return jnp.where(mask, 1.0, 0.0).astype(BF16)


def split16(values):
    high = jnp.floor(values * (1.0 / 128.0)) * 128.0
    return high.astype(BF16), (values - high).astype(BF16)


def offset(i):
    g, a, b = lax.div(i, 16), lax.div(lax.rem(i, 16), 4), lax.rem(i, 4)
    return b, lax.rem(lax.div(g, 4) + a + lax.div(b, 2), 2), lax.rem(a + b, 4), lax.rem(g + a + 3 * b, 4)


def kernel(
    ids_h, cnt_h, lids_h, self_h, node_owner, node_row, list_owner, list_row, features, centroids,
    w_self, w_neigh, w_query, w_out, w_context,
    emb_out, eb, cen,
    ids, cnt, lids_s, lids, self_f, no_v, nr_v, lo_v, lr_v, ft, ct, ws, wn, wq, wo, wc,
    btab, rq, rb, held, lo_rows, lr_rows, sb, gb, plb, obt, ns, na, s1, ps, pr, ob, load_sem, send_sem, recv_sem, ask_sem, row_sem,
):
    dp, x = lax.axis_index("dp"), lax.axis_index("mp")
    c, yz = lax.rem(dp, 2), lax.div(dp, 2)
    z, y = lax.rem(yz, 4), lax.div(yz, 4)
    me = dp * 4 + x

    def partners(g, sign):
        xs = [lax.rem(x + (sign * k) % 4, 4) for k in range(4)]
        zs = [lax.rem(z + (sign * k) % 4, 4) * 2 for k in range(4)]
        ys = [lax.rem(y + 16 + sign * (g + k), 4) * 8 for k in range(4)]
        cs = [lax.rem(c + lax.div(g, 4) + k, 2) for k in range(2)]
        return [
            (ys[(j // 4 + 3 * (j % 4)) % 4] + zs[(j // 4 + j % 4) % 4] + cs[(j // 4 + j % 4 // 2) % 2], xs[j % 4])
            for j in range(16)
        ]

    barrier = pltpu.get_barrier_semaphore()

    def greet(j_first):
        def body(g, _):
            for device in partners(g, 1)[j_first:]:
                pl.semaphore_signal(barrier, inc=1, device_id=device, device_id_type=MESH)
            return 0

        return body

    greet(1)(jnp.int32(0), 0)
    lax.fori_loop(1, 8, greet(0), 0)

    loads = [
        pltpu.make_async_copy(src, dst, load_sem.at[i])
        for i, (src, dst) in enumerate(
            [(node_owner, no_v), (node_row, nr_v), (list_owner, lo_v), (list_row, lr_v), (features, ft), (w_self, ws),
             (centroids, ct), (w_neigh, wn), (w_query, wq), (w_out, wo), (w_context, wc)]
        )
    ]
    small = [
        pltpu.make_async_copy(src, dst, load_sem.at[11 + i])
        for i, (src, dst) in enumerate([(ids_h, ids), (cnt_h, cnt), (lids_h.at[0], lids_s), (lids_h, lids), (self_h, self_f)])
    ]
    for load in loads[:2] + small + loads[2:]:
        load.start()

    def remote(src, dst, which, device, recv=None):
        return pltpu.make_async_remote_copy(
            src_ref=src, dst_ref=dst, send_sem=send_sem.at[which], recv_sem=recv_sem.at[which] if recv is None else recv,
            device_id=device, device_id_type=MESH,
        )

    def landed(ref, sem):
        pltpu.make_async_copy(ref, ref, sem).wait()

    for load in loads[:2] + small:
        load.wait()
    code = no_v[...] * 2048 + nr_v[...]
    btab[:, 0:128] = (lax.shift_right_logical(code, 9) - 256).astype(F32).astype(BF16)
    btab[:, 128:256] = (jnp.bitwise_and(code, 511) - 256).astype(F32).astype(BF16)
    ones = jnp.ones((128, 128), BF16)
    counts = column(cnt[...])
    ids_all = ids[...]
    lane = iota((256, 128), 1)
    lane_f = lane.astype(F32)
    tri = one_hot(iota((256, 256), 1) < iota((256, 256), 0))
    slot_row = iota((256, 1), 0)
    node = (lax.rem(slot_row, 32) + 1).astype(F32)
    counts8 = jnp.concatenate([counts] * 8, axis=0)
    four = range(4)
    idc = [jnp.concatenate([ids_all[:, 8 * q + j : 8 * q + j + 1] for j in range(8)], axis=0) for q in four]
    found = [dot(one_hot(iota((256, 2048), 1) == lax.shift_right_logical(idc[q], 7)), btab[...]) for q in four]
    sel = [lane == jnp.bitwise_and(idc[q], 127) for q in four]
    code = [
        (spread_pick(sel[q], found[q][:, 0:128], ones) + 256.0) * 512.0
        + (spread_pick(sel[q], found[q][:, 128:256], ones) + 256.0)
        for q in four
    ]
    owner = [jnp.floor(v * (1.0 / 2048.0)) for v in code]
    row = [v - o * 2048.0 for v, o in zip(code, owner)]
    high = [jnp.floor(v * (1.0 / 16.0)) * 16.0 for v in row]
    low = [v - h for v, h in zip(row, high)]
    mine = [lane_f == o for o in owner]
    hot = [one_hot(m) for m in mine]
    before = [dot(tri, h) for h in hot]
    sums = [jnp.sum(h.astype(F32), axis=0, keepdims=True) for h in hot]
    carry = [sum(sums[:q], jnp.zeros((1, 128), F32)) for q in four]
    rank = [spread_pick(mine[q], before[q] + carry[q], ones) for q in four]
    valid = [(lax.div(slot_row, 32) + 8 * q).astype(F32) < counts8 for q in four]
    x_high = [
        jnp.where(
            lane_f == rank[q], high[q], jnp.where(lane_f - 32.0 == rank[q], jnp.where(valid[q], node, 0.0), 0.0)
        ).astype(BF16)
        for q in four
    ]
    x_low = [jnp.where(lane_f == rank[q], low[q], 0.0).astype(BF16) for q in four]
    request = dot_first(jnp.concatenate(hot * 2, axis=0), jnp.concatenate(x_high + x_low, axis=0))

    loads[2].wait()
    loads[3].wait()

    def list_lookup(n, _):
        r = lax.div(lids_s[n], 128)
        lo_rows[pl.ds(n, 1), :] = lo_v[pl.ds(r, 1), :]
        lr_rows[pl.ds(n, 1), :] = lr_v[pl.ds(r, 1), :]
        return 0

    lax.fori_loop(0, 32, list_lookup, 0, unroll=8)
    lane32 = iota((32, 128), 1)
    lsel = lane32 == column(jnp.bitwise_and(lids[...], 127)).astype(jnp.int32)
    dest = pick(lsel, lo_rows[...].astype(F32))
    lrow = pick(lsel, lr_rows[...].astype(F32)) + 1.0
    lmine = lane32.astype(F32) == dest
    lhot = one_hot(lmine)
    lrank = pick(lmine, dot(one_hot(iota((32, 32), 1) < iota((32, 32), 0)), lhot))
    lhigh, llow = split16(lrow)
    lthere = (lane32 - 16).astype(F32) == lrank
    request = request + dot_first(lhot, jnp.where(lthere, lhigh.astype(F32), 0.0).astype(BF16))
    request = request + dot_first(lhot, jnp.where(lthere, llow.astype(F32), 0.0).astype(BF16))
    obt[...] = one_hot(iota((32, 256), 1).astype(F32) == dest + 128.0 * lrank)

    order_row, order_lane = iota((128, 128), 0), iota((128, 128), 1)
    kx, kc, kz, ky = offset(order_row)
    from_dp = (lax.rem(y + 4 - ky, 4) * 4 + lax.rem(z + 4 - kz, 4)) * 2 + lax.rem(c + kc, 2)
    asked = one_hot(order_lane == from_dp * 4 + lax.rem(x + 4 - kx, 4))
    high, low = split16(request)
    low = dot(asked, low)
    held[...] = low.astype(BF16)
    rq[:, 0, :] = dot(asked, high) + low

    pl.semaphore_wait(barrier, 127)

    def ask(j_first):
        def body(g, _):
            for j, device in list(enumerate(partners(g, -1)))[j_first:]:
                i = 16 * g + j
                remote(rq.at[i], rb.at[i], 0, device, ask_sem.at[g]).start()
            return 0

        return body

    pltpu.make_async_copy(rq.at[0], rb.at[0], ask_sem.at[0]).start()
    ask(1)(0, 0)
    lax.fori_loop(1, 8, ask(0), 0)

    ns[pl.ds(0, 32), :] = rms_rows(self_f[...].astype(F32)).astype(BF16)

    for i in range(1, 4):
        remote(ns.at[pl.ds(0, 32), :], ns.at[pl.ds(32 * i, 32), :], 2, (dp, lax.rem(x + i, 4))).start()

    spread = one_hot(lax.div(iota((256, 16), 0), 16) == iota((256, 16), 1))
    sub = lax.rem(iota((256, 128), 0), 16)
    loads[4].wait()

    def serve(j_first):
        def body(g, _):
            block = pl.ds(pl.multiple_of(16 * g, 16), 16)
            landed(rb.at[block], ask_sem.at[g])
            high, low = split16(rb[block, 0, :])
            index = pick(lane == sub, dot(spread, high) + dot(spread, low)).astype(jnp.int32)
            rows = dot(one_hot(iota((256, 2048), 1) == index), ft[...]).astype(BF16)
            sb[pl.ds(pl.multiple_of(256 * g, 256), 256), :] = rows
            for j, device in list(enumerate(partners(g, 1)))[j_first:]:
                part = pl.ds(pl.multiple_of(256 * g + 16 * j, 16), 16)
                remote(sb.at[part, :], gb.at[part, :], 3, device, row_sem.at[g]).start()
            return 0

        return body

    serve(1)(0, 0)
    own_rows = pltpu.make_async_copy(sb.at[pl.ds(0, 16), :], gb.at[pl.ds(0, 16), :], row_sem.at[0])
    own_rows.start()
    lax.fori_loop(1, 8, serve(0), 0)

    for g in range(8):
        node = pick(lane == sub + 32, dot(spread, held[pl.ds(16 * g, 16), :]))
        member = jnp.where(lane_f + 1.0 == node, 1.0, 0.0)
        plb[:, 256 * g : 256 * g + 256] = jnp.transpose(member)[0:32, :].astype(BF16)


    landed(ns.at[pl.ds(32, 96), :], recv_sem.at[2])
    loads[5].wait()
    s1[...] = dot(ns[...], ws[...])
    loads[6].wait()
    kx, kc, kz, ky = offset(order_lane)
    to_dp = (lax.rem(y + ky, 4) * 4 + lax.rem(z + kz, 4)) * 2 + lax.rem(c + kc, 2)
    by_source = one_hot(order_row == to_dp * 4 + lax.rem(x + kx, 4))
    high, low = split16(rb[:, 0, :])
    lists = dot(by_source, high) + dot(by_source, low)
    wanted = jnp.concatenate([lists[:, 16:17], lists[:, 17:18]], axis=0).astype(jnp.int32) - 1

    def centre(k, total):
        hot = one_hot(iota((256, 1024), 1) + 1024 * k == wanted)
        return total + dot(hot, ct[pl.ds(pl.multiple_of(1024 * k, 1024), 1024), :])

    centres = lax.fori_loop(0, 8, centre, jnp.zeros((256, 256), F32))
    cen[:, 0, :] = centres[0:128, :]
    cen[:, 1, :] = centres[128:256, :]

    total = jnp.zeros((32, 1024), F32)
    for g in range(8):
        landed(gb.at[pl.ds(256 * g, 256), :], row_sem.at[g])
        total = total + dot(plb[:, 256 * g : 256 * g + 256], gb[pl.ds(256 * g, 256), :])
    aggregate = (total / counts).astype(BF16)
    na[pl.ds(0, 32), :] = rms_rows(aggregate.astype(F32)).astype(BF16)
    for i in range(1, 4):
        remote(na.at[pl.ds(0, 32), :], na.at[pl.ds(32 * i, 32), :], 4, (dp, lax.rem(x + i, 4))).start()
    for load in loads[7:]:
        load.wait()
    landed(na.at[pl.ds(32, 96), :], recv_sem.at[4])
    hidden = jnp.maximum(s1[...] + dot(na[...], wn[...]), 0.0).astype(BF16)
    def share(columns, which):
        for i in range(1, 4):
            part = (pl.ds(32 * i, 32), columns)
            remote(ps.at[part], pr.at[part], which, (dp, lax.rem(x + 4 - i, 4))).start()

    def others(columns, which):
        landed(pr.at[pl.ds(32, 96), columns], recv_sem.at[which])
        return pr[pl.ds(32, 32), columns].astype(F32) + pr[pl.ds(64, 32), columns].astype(F32) + pr[pl.ds(96, 32), columns].astype(F32)

    for_query, for_head = pl.ds(0, 1024), pl.ds(1024, 256)
    to_query = dot(hidden, wq[...])
    ps[:, for_query] = to_query.astype(BF16)
    share(for_query, 5)
    to_head = dot(hidden, wo[...])
    ps[:, for_head] = to_head.astype(BF16)
    share(for_head, 1)
    queries = (to_query[0:32, :] + others(for_query, 5)).astype(BF16)
    scores = lax.dot_general(queries, gb[...], (((1,), (1,)), ((), ())), preferred_element_type=F32)
    gates = jnp.where(plb[...].astype(F32) > 0.5, jax.nn.sigmoid(scores * (1.0 / 32.0)), 0.0).astype(BF16)
    context = (dot(gates, gb[...]) / counts).astype(BF16)
    embedding = rms_rows((to_head[0:32, :] + others(for_head, 1)) + dot(context, wc[...])).astype(BF16)
    emb_out[...] = embedding

    slots = dot_first(obt[...], embedding)
    ob[:, 0, :] = slots[0:128, :]
    ob[:, 1, :] = slots[128:256, :]

    def tell(j_first):
        def body(g, _):
            for dp_to, x_to in partners(g, 1)[j_first:]:
                remote(ob.at[dp_to * 4 + x_to], eb.at[me], 6, (dp_to, x_to)).start()
            return 0

        return body

    tell(1)(0, 0)
    lax.fori_loop(1, 8, tell(0), 0)
    own_slots = pltpu.make_async_copy(ob.at[me], eb.at[me], recv_sem.at[6])
    own_slots.start()
    landed(eb, recv_sem.at[6])

    landed(rq.at[pl.ds(0, 127)], send_sem.at[0])
    landed(ns.at[pl.ds(0, 96), :], send_sem.at[2])
    landed(sb.at[pl.ds(16, 2032), :], send_sem.at[3])
    landed(na.at[pl.ds(0, 96), :], send_sem.at[4])
    landed(ps.at[pl.ds(32, 96), for_query], send_sem.at[5])
    landed(ps.at[pl.ds(32, 96), for_head], send_sem.at[1])
    landed(ob.at[pl.ds(0, 127)], send_sem.at[6])


def finish(emb_in, arrived, centres, emb_out, res_out):
    emb_out[...] = emb_in[...]
    res_out[...] = arrived[...] - centres[...]


def local(
    features_table, self_features, neighbour_ids, neighbour_counts, node_owner, node_row, list_ids, list_owner,
    list_row, centroids, w_self, w_neigh, w_query, w_out, w_context,
):
    vmem, anyw = (pl.BlockSpec(memory_space=m) for m in (pltpu.VMEM, pl.ANY))
    i32 = jnp.int32
    scratch = [
        ((2048, 128), i32), ((2048, 128), i32), ((8192, 128), i32), ((8192, 128), i32), ((2048, 1024), BF16),
        ((8192, 256), BF16), ((1024, 512), BF16), ((1024, 512), BF16), ((512, 1024), BF16), ((512, 256), BF16),
        ((1024, 256), BF16),
        ((2048, 256), BF16), ((128, 1, 128), F32), ((128, 1, 128), F32), ((128, 128), BF16), ((32, 128), i32), ((32, 128), i32),
        ((2048, 1024), BF16), ((2048, 1024), BF16), ((32, 2048), BF16), ((32, 256), BF16), ((128, 1024), BF16),
        ((128, 1024), BF16), ((128, 512), F32), ((128, 1280), BF16), ((128, 1280), BF16), ((128, 2, 256), F32),
    ]
    embedding, arrived, centres = pl.pallas_call(
        kernel,
        out_shape=(jax.ShapeDtypeStruct((32, 256), BF16),) + (jax.ShapeDtypeStruct((128, 2, 256), F32),) * 2,
        in_specs=[anyw] * 15,
        out_specs=(vmem, vmem, vmem),
        scratch_shapes=[pltpu.VMEM((32, 32), i32), pltpu.VMEM((1, 32), i32), pltpu.SMEM((32,), i32), pltpu.VMEM((1, 32), i32), pltpu.VMEM((32, 1024), BF16)]
        + [pltpu.VMEM(s, t) for s, t in scratch]
        + [pltpu.SemaphoreType.DMA((n,)) for n in (16, 8, 8, 8, 8)],
        compiler_params=pltpu.CompilerParams(collective_id=0, has_side_effects=True, vmem_limit_bytes=56 << 20),
    )(
        neighbour_ids, neighbour_counts.reshape(1, 32), list_ids.reshape(1, 32), self_features,
        node_owner.reshape(2048, 128), node_row.reshape(2048, 128), list_owner.reshape(8192, 128),
        list_row.reshape(8192, 128), features_table, centroids, w_self, w_neigh, w_query, w_out, w_context,
    )
    return pl.pallas_call(
        finish,
        out_shape=(jax.ShapeDtypeStruct((32, 256), BF16), jax.ShapeDtypeStruct((128, 2, 256), F32)),
        in_specs=[vmem] * 3,
        out_specs=(vmem, vmem),
    )(embedding, arrived, centres)


def solution(mesh):
    placed = (
        P(("dp", "mp"), None),
        P(("dp", "mp"), None),
        P(("dp", "mp"), None),
        P(("dp", "mp")),
        P(),
        P(),
        P(("dp", "mp")),
        P(),
        P(),
        P(("dp", "mp"), None),
        P(None, "mp"),
        P(None, "mp"),
        P("mp", None),
        P("mp", None),
        P(),
    )
    return jax.shard_map(
        local,
        mesh=mesh,
        in_specs=placed,
        out_specs=(P(("dp", "mp"), None), P(("dp", "mp"), None, None)),
        check_vma=False,
    )
```

```python
import math

import jax
import jax.numpy as jnp
from jax import lax
from jax.experimental import pallas as pl
from jax.experimental.pallas import tpu as pltpu
from jax.sharding import PartitionSpec as P

MESH = pl.DeviceIdType.MESH
F32, BF16 = jnp.float32, jnp.bfloat16


def dot(a, b):
    return jnp.dot(a, b, preferred_element_type=F32)


def dot_first(a, b):
    return lax.dot_general(a, b, (((0,), (0,)), ((), ())), preferred_element_type=F32)


def rms_rows(values):
    return values * lax.rsqrt(jnp.mean(values * values, axis=-1, keepdims=True) + 1e-06)


def iota(shape, dim):
    return lax.broadcasted_iota(jnp.int32, shape, dim)


def pick(mask, values):
    return jnp.sum(jnp.where(mask, values, 0.0), axis=1, keepdims=True)


def spread_pick(mask, values, ones):
    return dot(jnp.where(mask, values, 0.0).astype(BF16), ones)


def column(row):
    return jnp.sum(jnp.where(iota((32, 32), 0) == iota((32, 32), 1), row.astype(F32), 0.0), axis=1, keepdims=True)


def one_hot(mask):
    return jnp.where(mask, 1.0, 0.0).astype(BF16)


def split16(values):
    high = jnp.floor(values * (1.0 / 128.0)) * 128.0
    return high.astype(BF16), (values - high).astype(BF16)


def offset(i):
    g, a, b = lax.div(i, 16), lax.div(lax.rem(i, 16), 4), lax.rem(i, 4)
    return b, lax.rem(lax.div(g, 4) + a + lax.div(b, 2), 2), lax.rem(a + b, 4), lax.rem(g + a + 3 * b, 4)


def kernel(
    ids_h, cnt_h, lids_h, self_h, node_owner, node_row, list_owner, list_row, features, centroids,
    w_self, w_neigh, w_query, w_out, w_context,
    emb_out, eb, cen,
    ids, cnt, lids_s, lids, self_f, no_v, nr_v, lo_v, lr_v, ft, ct, ws, wn, wq, wo, wc,
    btab, rq, rb, rl, ll, held, lo_rows, lr_rows, sb, gb, plb, obt, ns, na, s1, ps, pr, ob, cen_v, load_sem, send_sem, recv_sem, ask_sem, row_sem,
):
    dp, x = lax.axis_index("dp"), lax.axis_index("mp")
    c, yz = lax.rem(dp, 2), lax.div(dp, 2)
    z, y = lax.rem(yz, 4), lax.div(yz, 4)
    me = dp * 4 + x

    def turned(at, size, scale):
        return [lax.rem(at + k, size) * scale for k in range(size)]

    all_x, all_c, all_z, all_y = turned(x, 4, 1), turned(c, 2, 1), turned(z, 4, 2), turned(y, 4, 8)

    def partner(i, sign):
        g, a, b = i // 16, i % 16 // 4, i % 4
        y_z = all_y[sign * (g + a + 3 * b) % 4] + all_z[sign * (a + b) % 4]
        return y_z + all_c[(g // 4 + a + b // 2) % 2], all_x[sign * b % 4]

    def partners(g):
        ys, cs = turned(y + g, 4, 8), turned(c + lax.div(g, 4), 2, 1)
        return [
            (ys[(j // 4 + 3 * (j % 4)) % 4] + all_z[(j // 4 + j % 4) % 4] + cs[(j // 4 + j % 4 // 2) % 2], all_x[j % 4])
            for j in range(16)
        ]

    loads = [
        pltpu.make_async_copy(src, dst, load_sem.at[i])
        for i, (src, dst) in enumerate(
            [(node_owner, no_v), (node_row, nr_v), (list_owner, lo_v), (list_row, lr_v), (features, ft), (w_self, ws),
             (centroids, ct), (w_neigh, wn), (w_query, wq), (w_out, wo), (w_context, wc)]
        )
    ]
    small = [
        pltpu.make_async_copy(src, dst, load_sem.at[11 + i])
        for i, (src, dst) in enumerate([(ids_h, ids), (cnt_h, cnt), (lids_h.at[0], lids_s), (lids_h, lids), (self_h, self_f)])
    ]
    for load in small[:2] + loads[:2]:
        load.start()

    barrier = pltpu.get_barrier_semaphore()

    for i in range(1, 128):
        pl.semaphore_signal(barrier, inc=1, device_id=partner(i, 1), device_id_type=MESH)

    for load in loads[4:5] + small[2:] + loads[2:4] + loads[5:]:
        load.start()


    def remote(src, dst, which, device, recv=None):
        return pltpu.make_async_remote_copy(
            src_ref=src, dst_ref=dst, send_sem=send_sem.at[which], recv_sem=recv_sem.at[which] if recv is None else recv,
            device_id=device, device_id_type=MESH,
        )

    def landed(ref, sem):
        pltpu.make_async_copy(ref, ref, sem).wait()

    def sent_from(i):
        kx, kc, kz, ky = offset(i)
        y_z = lax.rem(y + 4 - ky, 4) * 4 + lax.rem(z + 4 - kz, 4)
        return ((y_z * 2 + lax.rem(c + kc, 2)) * 4 + lax.rem(x + 4 - kx, 4)).astype(F32)

    lane = iota((256, 128), 1)
    lane_f = lane.astype(F32)
    partner_lane = sent_from(lane)
    tri = one_hot(iota((256, 256), 1) < iota((256, 256), 0))
    ones = jnp.ones((128, 128), BF16)
    weigh = jnp.where(iota((256, 128), 0) < 128, 512.0, 1.0).astype(BF16)
    slot_row = iota((256, 1), 0)
    node = (lax.rem(slot_row, 32) + 1).astype(F32)
    for load in small[:2] + loads[:2]:
        load.wait()
    code = no_v[...] * 2048 + nr_v[...]
    btab[:, 0:128] = (lax.shift_right_logical(code, 9) - 256).astype(F32).astype(BF16)
    btab[:, 128:256] = (jnp.bitwise_and(code, 511) - 256).astype(F32).astype(BF16)
    counts = column(cnt[...])
    ids_all = ids[...]
    counts8 = jnp.concatenate([counts] * 8, axis=0)
    four = range(4)
    idc = [jnp.concatenate([ids_all[:, 8 * q + j : 8 * q + j + 1] for j in range(8)], axis=0) for q in four]
    found = [dot(one_hot(iota((256, 2048), 1) == lax.shift_right_logical(idc[q], 7)), btab[...]) for q in four]
    sel = [jnp.bitwise_and(iota((256, 256), 1), 127) == jnp.bitwise_and(idc[q], 127) for q in four]
    code = [dot(jnp.where(sel[q], found[q], 0.0).astype(BF16), weigh) + float(256 * 512 + 256) for q in four]
    owner = [jnp.floor(v * (1.0 / 2048.0)) for v in code]
    row = [v - o * 2048.0 for v, o in zip(code, owner)]
    high = [jnp.floor(v * (1.0 / 16.0)) * 16.0 for v in row]
    low = [v - h for v, h in zip(row, high)]
    mine = [partner_lane == o for o in owner]
    hot = [one_hot(m) for m in mine]
    before = [dot(tri, h) for h in hot]
    sums = [jnp.sum(h.astype(F32), axis=0, keepdims=True) for h in hot]
    carry = [sum(sums[:q], jnp.zeros((1, 128), F32)) for q in four]
    rank = [spread_pick(mine[q], before[q] + carry[q], ones) for q in four]
    valid = [(lax.div(slot_row, 32) + 8 * q).astype(F32) < counts8 for q in four]
    x_high = [
        jnp.where(
            lane_f == rank[q], high[q], jnp.where(lane_f - 32.0 == rank[q], jnp.where(valid[q], node, 0.0), 0.0)
        ).astype(BF16)
        for q in four
    ]
    x_low = [jnp.where(lane_f == rank[q], low[q], 0.0).astype(BF16) for q in four]
    request = dot_first(jnp.concatenate(hot * 2, axis=0), jnp.concatenate(x_high + x_low, axis=0))

    rq[:, 0, :] = request
    held[...] = split16(request)[1]

    pl.semaphore_wait(barrier, 127)

    for i in range(1, 128):
        remote(rq.at[i], rb.at[i], 0, partner(i, -1), ask_sem.at[i // 16]).start()
    pltpu.make_async_copy(rq.at[0], rb.at[0], ask_sem.at[0]).start()

    small[4].wait()
    ns[pl.ds(0, 32), :] = rms_rows(self_f[...].astype(F32)).astype(BF16)

    for i in range(1, 4):
        remote(ns.at[pl.ds(0, 32), :], ns.at[pl.ds(32 * i, 32), :], 2, (dp, lax.rem(x + i, 4))).start()

    spread = one_hot(lax.div(iota((256, 16), 0), 16) == iota((256, 16), 1))
    sub = lax.rem(iota((256, 128), 0), 16)
    loads[4].wait()

    def serve(j_first):
        def body(g, _):
            block = pl.ds(pl.multiple_of(16 * g, 16), 16)
            landed(rb.at[block], ask_sem.at[g])
            high, low = split16(rb[block, 0, :])
            index = pick(lane == sub, dot(spread, high) + dot(spread, low)).astype(jnp.int32)
            rows = dot(one_hot(iota((256, 2048), 1) == index), ft[...]).astype(BF16)
            sb[pl.ds(pl.multiple_of(256 * g, 256), 256), :] = rows
            for j, device in list(enumerate(partners(g)))[j_first:]:
                part = pl.ds(pl.multiple_of(256 * g + 16 * j, 16), 16)
                remote(sb.at[part, :], gb.at[part, :], 3, device, row_sem.at[g]).start()
            return 0

        return body

    serve(1)(0, 0)
    own_rows = pltpu.make_async_copy(sb.at[pl.ds(0, 16), :], gb.at[pl.ds(0, 16), :], row_sem.at[0])
    own_rows.start()
    for load in small[2:4] + loads[2:4]:
        load.wait()

    def list_lookup(n, _):
        r = lax.div(lids_s[n], 128)
        lo_rows[pl.ds(n, 1), :] = lo_v[pl.ds(r, 1), :]
        lr_rows[pl.ds(n, 1), :] = lr_v[pl.ds(r, 1), :]
        return 0

    lax.fori_loop(0, 32, list_lookup, 0, unroll=8)
    lane32 = iota((32, 128), 1)
    lsel = lane32 == column(jnp.bitwise_and(lids[...], 127)).astype(jnp.int32)
    dest = pick(lsel, lo_rows[...].astype(F32))
    lrow = pick(lsel, lr_rows[...].astype(F32)) + 1.0
    lmine = sent_from(lane32) == dest
    lhot = one_hot(lmine)
    lrank = pick(lmine, dot(one_hot(iota((32, 32), 1) < iota((32, 32), 0)), lhot))
    lhigh, llow = split16(lrow)
    lthere = (lane32 - 16).astype(F32) == lrank
    rl[:, 0, :] = dot_first(lhot, jnp.where(lthere, lhigh.astype(F32), 0.0).astype(BF16)) + dot_first(
        lhot, jnp.where(lthere, llow.astype(F32), 0.0).astype(BF16)
    )
    for i in range(1, 128):
        remote(rl.at[i], ll.at[i], 7, partner(i, -1)).start()
    pltpu.make_async_copy(rl.at[0], ll.at[0], recv_sem.at[7]).start()
    obt[...] = one_hot(iota((32, 256), 1).astype(F32) == dest + 128.0 * lrank)

    lax.fori_loop(1, 8, serve(0), 0)

    for g in range(8):
        node = pick(lane == sub + 32, dot(spread, held[pl.ds(16 * g, 16), :]))
        member = jnp.where(lane_f + 1.0 == node, 1.0, 0.0)
        plb[:, 256 * g : 256 * g + 256] = jnp.transpose(member)[0:32, :].astype(BF16)


    landed(ns.at[pl.ds(32, 96), :], recv_sem.at[2])
    loads[5].wait()
    s1[...] = dot(ns[...], ws[...])
    loads[6].wait()
    order_row, order_lane = iota((128, 128), 0), iota((128, 128), 1)
    kx, kc, kz, ky = offset(order_lane)
    to_dp = (lax.rem(y + ky, 4) * 4 + lax.rem(z + kz, 4)) * 2 + lax.rem(c + kc, 2)
    by_source = one_hot(order_row == to_dp * 4 + lax.rem(x + kx, 4))
    landed(ll, recv_sem.at[7])
    high, low = split16(ll[:, 0, :])
    lists = dot(by_source, high) + dot(by_source, low)
    wanted = jnp.concatenate([lists[:, 16:17], lists[:, 17:18]], axis=0).astype(jnp.int32) - 1

    def centre(k, total):
        hot = one_hot(iota((256, 1024), 1) + 1024 * k == wanted)
        return total + dot(hot, ct[pl.ds(pl.multiple_of(1024 * k, 1024), 1024), :])

    centres = lax.fori_loop(0, 8, centre, jnp.zeros((256, 256), F32))
    cen_v[:, 0, :] = centres[0:128, :]
    cen_v[:, 1, :] = centres[128:256, :]
    keep = pltpu.make_async_copy(cen_v, cen, recv_sem.at[0])
    keep.start()

    total = jnp.zeros((32, 1024), F32)
    for g in range(8):
        landed(gb.at[pl.ds(256 * g, 256), :], row_sem.at[g])
        total = total + dot(plb[:, 256 * g : 256 * g + 256], gb[pl.ds(256 * g, 256), :])
    aggregate = (total / counts).astype(BF16)
    na[pl.ds(0, 32), :] = rms_rows(aggregate.astype(F32)).astype(BF16)
    for i in range(1, 4):
        remote(na.at[pl.ds(0, 32), :], na.at[pl.ds(32 * i, 32), :], 4, (dp, lax.rem(x + i, 4))).start()
    for load in loads[7:]:
        load.wait()
    landed(na.at[pl.ds(32, 96), :], recv_sem.at[4])
    hidden = jnp.maximum(s1[...] + dot(na[...], wn[...]), 0.0).astype(BF16)
    def share(columns, which):
        for i in range(1, 4):
            part = (pl.ds(32 * i, 32), columns)
            remote(ps.at[part], pr.at[part], which, (dp, lax.rem(x + 4 - i, 4))).start()

    def others(columns, which):
        landed(pr.at[pl.ds(32, 96), columns], recv_sem.at[which])
        return pr[pl.ds(32, 32), columns].astype(F32) + pr[pl.ds(64, 32), columns].astype(F32) + pr[pl.ds(96, 32), columns].astype(F32)

    for_query, for_head = pl.ds(0, 1024), pl.ds(1024, 256)
    to_query = dot(hidden, wq[...])
    ps[:, for_query] = to_query.astype(BF16)
    share(for_query, 5)
    to_head = dot(hidden, wo[...])
    ps[:, for_head] = to_head.astype(BF16)
    share(for_head, 1)
    queries = (to_query[0:32, :] + others(for_query, 5)).astype(BF16)
    scores = lax.dot_general(queries, gb[...], (((1,), (1,)), ((), ())), preferred_element_type=F32)
    gates = jnp.where(plb[...].astype(F32) > 0.5, jax.nn.sigmoid(scores * (1.0 / 32.0)), 0.0).astype(BF16)
    context = (dot(gates, gb[...]) / counts).astype(BF16)
    embedding = rms_rows((to_head[0:32, :] + others(for_head, 1)) + dot(context, wc[...])).astype(BF16)
    emb_out[...] = embedding

    slots = dot_first(obt[...], embedding)
    ob[:, 0, :] = slots[0:128, :]
    ob[:, 1, :] = slots[128:256, :]

    for i in range(1, 128):
        dp_to, x_to = partner(i, 1)
        remote(ob.at[dp_to * 4 + x_to], eb.at[me], 6, (dp_to, x_to)).start()
    own_slots = pltpu.make_async_copy(ob.at[me], eb.at[me], recv_sem.at[6])
    own_slots.start()
    landed(eb, recv_sem.at[6])

    keep.wait()
    landed(rq.at[pl.ds(0, 127)], send_sem.at[0])
    landed(ns.at[pl.ds(0, 96), :], send_sem.at[2])
    landed(sb.at[pl.ds(16, 2032), :], send_sem.at[3])
    landed(na.at[pl.ds(0, 96), :], send_sem.at[4])
    landed(ps.at[pl.ds(32, 96), for_query], send_sem.at[5])
    landed(ps.at[pl.ds(32, 96), for_head], send_sem.at[1])
    landed(ob.at[pl.ds(0, 127)], send_sem.at[6])
    landed(rl.at[pl.ds(0, 127)], send_sem.at[7])


def finish(emb_in, arrived, centres, emb_out, res_out):
    emb_out[...] = emb_in[...]
    res_out[...] = arrived[...] - centres[...]


def local(
    features_table, self_features, neighbour_ids, neighbour_counts, node_owner, node_row, list_ids, list_owner,
    list_row, centroids, w_self, w_neigh, w_query, w_out, w_context,
):
    vmem, anyw = (pl.BlockSpec(memory_space=m) for m in (pltpu.VMEM, pl.ANY))
    i32 = jnp.int32
    scratch = [
        ((2048, 128), i32), ((2048, 128), i32), ((8192, 128), i32), ((8192, 128), i32), ((2048, 1024), BF16),
        ((8192, 256), BF16), ((1024, 512), BF16), ((1024, 512), BF16), ((512, 1024), BF16), ((512, 256), BF16),
        ((1024, 256), BF16),
        ((2048, 256), BF16), ((128, 1, 128), F32), ((128, 1, 128), F32), ((128, 1, 128), F32), ((128, 1, 128), F32), ((128, 128), BF16), ((32, 128), i32), ((32, 128), i32),
        ((2048, 1024), BF16), ((2048, 1024), BF16), ((32, 2048), BF16), ((32, 256), BF16), ((128, 1024), BF16),
        ((128, 1024), BF16), ((128, 512), F32), ((128, 1280), BF16), ((128, 1280), BF16), ((128, 2, 256), F32), ((128, 2, 256), F32),
    ]
    embedding, arrived, centres = pl.pallas_call(
        kernel,
        out_shape=(jax.ShapeDtypeStruct((32, 256), BF16),) + (jax.ShapeDtypeStruct((128, 2, 256), F32),) * 2,
        in_specs=[anyw] * 15,
        out_specs=(vmem, vmem, anyw),
        scratch_shapes=[pltpu.VMEM((32, 32), i32), pltpu.VMEM((1, 32), i32), pltpu.SMEM((32,), i32), pltpu.VMEM((1, 32), i32), pltpu.VMEM((32, 1024), BF16)]
        + [pltpu.VMEM(s, t) for s, t in scratch]
        + [pltpu.SemaphoreType.DMA((n,)) for n in (16, 8, 8, 8, 8)],
        compiler_params=pltpu.CompilerParams(collective_id=0, has_side_effects=True, vmem_limit_bytes=56 << 20),
    )(
        neighbour_ids, neighbour_counts.reshape(1, 32), list_ids.reshape(1, 32), self_features,
        node_owner.reshape(2048, 128), node_row.reshape(2048, 128), list_owner.reshape(8192, 128),
        list_row.reshape(8192, 128), features_table, centroids, w_self, w_neigh, w_query, w_out, w_context,
    )
    return pl.pallas_call(
        finish,
        out_shape=(jax.ShapeDtypeStruct((32, 256), BF16), jax.ShapeDtypeStruct((128, 2, 256), F32)),
        in_specs=[vmem] * 3,
        out_specs=(vmem, vmem),
    )(embedding, arrived, centres)


def solution(mesh):
    placed = (
        P(("dp", "mp"), None),
        P(("dp", "mp"), None),
        P(("dp", "mp"), None),
        P(("dp", "mp")),
        P(),
        P(),
        P(("dp", "mp")),
        P(),
        P(),
        P(("dp", "mp"), None),
        P(None, "mp"),
        P(None, "mp"),
        P("mp", None),
        P("mp", None),
        P(),
    )
    return jax.shard_map(
        local,
        mesh=mesh,
        in_specs=placed,
        out_specs=(P(("dp", "mp"), None), P(("dp", "mp"), None, None)),
        check_vma=False,
    )
```

```python
import math

import jax
import jax.numpy as jnp
from jax import lax
from jax.experimental import pallas as pl
from jax.experimental.pallas import tpu as pltpu
from jax.sharding import PartitionSpec as P

MESH = pl.DeviceIdType.MESH
F32, BF16 = jnp.float32, jnp.bfloat16


def dot(a, b):
    return jnp.dot(a, b, preferred_element_type=F32)


def dot_first(a, b):
    return lax.dot_general(a, b, (((0,), (0,)), ((), ())), preferred_element_type=F32)


def rms_rows(values):
    return values * lax.rsqrt(jnp.mean(values * values, axis=-1, keepdims=True) + 1e-06)


def iota(shape, dim):
    return lax.broadcasted_iota(jnp.int32, shape, dim)


def pick(mask, values):
    return jnp.sum(jnp.where(mask, values, 0.0), axis=1, keepdims=True)


def spread_pick(mask, values, ones):
    return dot(jnp.where(mask, values, 0.0).astype(BF16), ones)


def column(row):
    return jnp.sum(jnp.where(iota((32, 32), 0) == iota((32, 32), 1), row.astype(F32), 0.0), axis=1, keepdims=True)


def one_hot(mask):
    return jnp.where(mask, 1.0, 0.0).astype(BF16)


def split16(values):
    high = jnp.floor(values * (1.0 / 128.0)) * 128.0
    return high.astype(BF16), (values - high).astype(BF16)


def offset(i):
    g, a, b = lax.div(i, 16), lax.div(lax.rem(i, 16), 4), lax.rem(i, 4)
    return b, lax.rem(lax.div(g, 4) + a + lax.div(b, 2), 2), lax.rem(a + b, 4), lax.rem(g + a + 3 * b, 4)


def kernel(
    ids_h, cnt_h, lids_h, self_h, node_owner, node_row, list_owner, list_row, features, centroids,
    w_self, w_neigh, w_query, w_out, w_context,
    emb_out, eb, cen,
    ids, cnt, lids_s, lids, self_f, no_v, nr_v, lo_v, lr_v, ft, ct, ws, wn, wq, wo, wc,
    btab, rq, rb, rl, ll, held, lo_rows, lr_rows, sb, gb, plb, obt, ns, na, s1, ps, pr, ob, cen_v, load_sem, send_sem, recv_sem, ask_sem, row_sem,
):
    dp, x = lax.axis_index("dp"), lax.axis_index("mp")
    c, yz = lax.rem(dp, 2), lax.div(dp, 2)
    z, y = lax.rem(yz, 4), lax.div(yz, 4)
    me = dp * 4 + x

    def turned(at, size, scale):
        return [lax.rem(at + k, size) * scale for k in range(size)]

    all_x, all_c, all_z, all_y = turned(x, 4, 1), turned(c, 2, 1), turned(z, 4, 2), turned(y, 4, 8)

    def partner(i, sign):
        g, a, b = i // 16, i % 16 // 4, i % 4
        y_z = all_y[sign * (g + a + 3 * b) % 4] + all_z[sign * (a + b) % 4]
        return y_z + all_c[(g // 4 + a + b // 2) % 2], all_x[sign * b % 4]

    def partners(g):
        ys, cs = turned(y + g, 4, 8), turned(c + lax.div(g, 4), 2, 1)
        return [
            (ys[(j // 4 + 3 * (j % 4)) % 4] + all_z[(j // 4 + j % 4) % 4] + cs[(j // 4 + j % 4 // 2) % 2], all_x[j % 4])
            for j in range(16)
        ]

    loads = [
        pltpu.make_async_copy(src, dst, load_sem.at[i])
        for i, (src, dst) in enumerate(
            [(node_owner, no_v), (node_row, nr_v), (list_owner, lo_v), (list_row, lr_v), (features, ft), (w_self, ws),
             (centroids, ct), (w_neigh, wn), (w_query, wq), (w_out, wo), (w_context, wc)]
        )
    ]
    small = [
        pltpu.make_async_copy(src, dst, load_sem.at[11 + i])
        for i, (src, dst) in enumerate([(ids_h, ids), (cnt_h, cnt), (lids_h.at[0], lids_s), (lids_h, lids), (self_h, self_f)])
    ]
    for load in small[:2] + loads[:2]:
        load.start()

    barrier = pltpu.get_barrier_semaphore()

    for i in range(1, 128):
        pl.semaphore_signal(barrier, inc=1, device_id=partner(i, 1), device_id_type=MESH)

    for load in loads[4:5] + small[2:]:
        load.start()


    def remote(src, dst, which, device, recv=None):
        return pltpu.make_async_remote_copy(
            src_ref=src, dst_ref=dst, send_sem=send_sem.at[which], recv_sem=recv_sem.at[which] if recv is None else recv,
            device_id=device, device_id_type=MESH,
        )

    def landed(ref, sem):
        pltpu.make_async_copy(ref, ref, sem).wait()

    def sent_from(i):
        kx, kc, kz, ky = offset(i)
        y_z = lax.rem(y + 4 - ky, 4) * 4 + lax.rem(z + 4 - kz, 4)
        return ((y_z * 2 + lax.rem(c + kc, 2)) * 4 + lax.rem(x + 4 - kx, 4)).astype(F32)

    lane = iota((256, 128), 1)
    lane_f = lane.astype(F32)
    partner_lane = sent_from(lane)
    tri = one_hot(iota((256, 256), 1) < iota((256, 256), 0))
    ones = jnp.ones((128, 128), BF16)
    weigh = jnp.where(iota((256, 128), 0) < 128, 512.0, 1.0).astype(BF16)
    slot_row = iota((256, 1), 0)
    node = (lax.rem(slot_row, 32) + 1).astype(F32)
    for load in small[:2] + loads[:2]:
        load.wait()
    code = no_v[...] * 2048 + nr_v[...]
    btab[:, 0:128] = (lax.shift_right_logical(code, 9) - 256).astype(F32).astype(BF16)
    btab[:, 128:256] = (jnp.bitwise_and(code, 511) - 256).astype(F32).astype(BF16)
    counts = column(cnt[...])
    ids_all = ids[...]
    counts8 = jnp.concatenate([counts] * 8, axis=0)
    four = range(4)
    idc = [jnp.concatenate([ids_all[:, 8 * q + j : 8 * q + j + 1] for j in range(8)], axis=0) for q in four]
    found = [dot(one_hot(iota((256, 2048), 1) == lax.shift_right_logical(idc[q], 7)), btab[...]) for q in four]
    sel = [jnp.bitwise_and(iota((256, 256), 1), 127) == jnp.bitwise_and(idc[q], 127) for q in four]
    code = [dot(jnp.where(sel[q], found[q], 0.0).astype(BF16), weigh) + float(256 * 512 + 256) for q in four]
    owner = [jnp.floor(v * (1.0 / 2048.0)) for v in code]
    row = [v - o * 2048.0 for v, o in zip(code, owner)]
    high = [jnp.floor(v * (1.0 / 16.0)) * 16.0 for v in row]
    low = [v - h for v, h in zip(row, high)]
    mine = [partner_lane == o for o in owner]
    hot = [one_hot(m) for m in mine]
    before = [dot(tri, h) for h in hot]
    sums = [jnp.sum(h.astype(F32), axis=0, keepdims=True) for h in hot]
    carry = [sum(sums[:q], jnp.zeros((1, 128), F32)) for q in four]
    rank = [spread_pick(mine[q], before[q] + carry[q], ones) for q in four]
    valid = [(lax.div(slot_row, 32) + 8 * q).astype(F32) < counts8 for q in four]
    x_high = [
        jnp.where(
            lane_f == rank[q], high[q], jnp.where(lane_f - 32.0 == rank[q], jnp.where(valid[q], node, 0.0), 0.0)
        ).astype(BF16)
        for q in four
    ]
    x_low = [jnp.where(lane_f == rank[q], low[q], 0.0).astype(BF16) for q in four]
    request = dot_first(jnp.concatenate(hot * 2, axis=0), jnp.concatenate(x_high + x_low, axis=0))

    rq[:, 0, :] = request
    held[...] = split16(request)[1]

    pl.semaphore_wait(barrier, 127)

    for i in range(1, 128):
        remote(rq.at[i], rb.at[i], 0, partner(i, -1), ask_sem.at[i // 16]).start()
    pltpu.make_async_copy(rq.at[0], rb.at[0], ask_sem.at[0]).start()
    for load in loads[2:4]:
        load.start()

    small[4].wait()
    ns[pl.ds(0, 32), :] = rms_rows(self_f[...].astype(F32)).astype(BF16)

    for i in range(1, 4):
        remote(ns.at[pl.ds(0, 32), :], ns.at[pl.ds(32 * i, 32), :], 2, (dp, lax.rem(x + i, 4))).start()

    spread = one_hot(lax.div(iota((256, 16), 0), 16) == iota((256, 16), 1))
    sub = lax.rem(iota((256, 128), 0), 16)
    loads[4].wait()

    def serve(j_first):
        def body(g, _):
            block = pl.ds(pl.multiple_of(16 * g, 16), 16)
            landed(rb.at[block], ask_sem.at[g])
            high, low = split16(rb[block, 0, :])
            index = pick(lane == sub, dot(spread, high) + dot(spread, low)).astype(jnp.int32)
            rows = dot(one_hot(iota((256, 2048), 1) == index), ft[...]).astype(BF16)
            sb[pl.ds(pl.multiple_of(256 * g, 256), 256), :] = rows
            for j, device in list(enumerate(partners(g)))[j_first:]:
                part = pl.ds(pl.multiple_of(256 * g + 16 * j, 16), 16)
                remote(sb.at[part, :], gb.at[part, :], 3, device, row_sem.at[g]).start()
            return 0

        return body

    serve(1)(0, 0)
    own_rows = pltpu.make_async_copy(sb.at[pl.ds(0, 16), :], gb.at[pl.ds(0, 16), :], row_sem.at[0])
    own_rows.start()
    for load in small[2:4] + loads[2:4]:
        load.wait()

    def list_lookup(n, _):
        r = lax.div(lids_s[n], 128)
        lo_rows[pl.ds(n, 1), :] = lo_v[pl.ds(r, 1), :]
        lr_rows[pl.ds(n, 1), :] = lr_v[pl.ds(r, 1), :]
        return 0

    lax.fori_loop(0, 32, list_lookup, 0, unroll=8)
    lane32 = iota((32, 128), 1)
    lsel = lane32 == column(jnp.bitwise_and(lids[...], 127)).astype(jnp.int32)
    dest = pick(lsel, lo_rows[...].astype(F32))
    lrow = pick(lsel, lr_rows[...].astype(F32)) + 1.0
    lmine = sent_from(lane32) == dest
    lhot = one_hot(lmine)
    lrank = pick(lmine, dot(one_hot(iota((32, 32), 1) < iota((32, 32), 0)), lhot))
    lhigh, llow = split16(lrow)
    lthere = (lane32 - 16).astype(F32) == lrank
    rl[:, 0, :] = dot_first(lhot, jnp.where(lthere, lhigh.astype(F32), 0.0).astype(BF16)) + dot_first(
        lhot, jnp.where(lthere, llow.astype(F32), 0.0).astype(BF16)
    )
    for i in range(1, 128):
        remote(rl.at[i], ll.at[i], 7, partner(i, -1)).start()
    pltpu.make_async_copy(rl.at[0], ll.at[0], recv_sem.at[7]).start()
    obt[...] = one_hot(iota((32, 256), 1).astype(F32) == dest + 128.0 * lrank)

    for load in loads[5:]:
        load.start()
    lax.fori_loop(1, 8, serve(0), 0)

    for g in range(8):
        node = pick(lane == sub + 32, dot(spread, held[pl.ds(16 * g, 16), :]))
        member = jnp.where(lane_f + 1.0 == node, 1.0, 0.0)
        plb[:, 256 * g : 256 * g + 256] = jnp.transpose(member)[0:32, :].astype(BF16)


    landed(ns.at[pl.ds(32, 96), :], recv_sem.at[2])
    loads[5].wait()
    s1[...] = dot(ns[...], ws[...])
    loads[6].wait()
    order_row, order_lane = iota((128, 128), 0), iota((128, 128), 1)
    kx, kc, kz, ky = offset(order_lane)
    to_dp = (lax.rem(y + ky, 4) * 4 + lax.rem(z + kz, 4)) * 2 + lax.rem(c + kc, 2)
    by_source = one_hot(order_row == to_dp * 4 + lax.rem(x + kx, 4))
    landed(ll, recv_sem.at[7])
    high, low = split16(ll[:, 0, :])
    lists = dot(by_source, high) + dot(by_source, low)
    wanted = jnp.concatenate([lists[:, 16:17], lists[:, 17:18]], axis=0).astype(jnp.int32) - 1

    def centre(k, total):
        hot = one_hot(iota((256, 1024), 1) + 1024 * k == wanted)
        return total + dot(hot, ct[pl.ds(pl.multiple_of(1024 * k, 1024), 1024), :])

    centres = lax.fori_loop(0, 8, centre, jnp.zeros((256, 256), F32))
    cen_v[:, 0, :] = centres[0:128, :]
    cen_v[:, 1, :] = centres[128:256, :]
    keep = pltpu.make_async_copy(cen_v, cen, recv_sem.at[0])
    keep.start()

    total = jnp.zeros((32, 1024), F32)
    for g in range(8):
        landed(gb.at[pl.ds(256 * g, 256), :], row_sem.at[g])
        total = total + dot(plb[:, 256 * g : 256 * g + 256], gb[pl.ds(256 * g, 256), :])
    aggregate = (total / counts).astype(BF16)
    na[pl.ds(0, 32), :] = rms_rows(aggregate.astype(F32)).astype(BF16)
    for i in range(1, 4):
        remote(na.at[pl.ds(0, 32), :], na.at[pl.ds(32 * i, 32), :], 4, (dp, lax.rem(x + i, 4))).start()
    for load in loads[7:]:
        load.wait()
    landed(na.at[pl.ds(32, 96), :], recv_sem.at[4])
    hidden = jnp.maximum(s1[...] + dot(na[...], wn[...]), 0.0).astype(BF16)
    def share(columns, which):
        for i in range(1, 4):
            part = (pl.ds(32 * i, 32), columns)
            remote(ps.at[part], pr.at[part], which, (dp, lax.rem(x + 4 - i, 4))).start()

    def others(columns, which):
        landed(pr.at[pl.ds(32, 96), columns], recv_sem.at[which])
        return pr[pl.ds(32, 32), columns].astype(F32) + pr[pl.ds(64, 32), columns].astype(F32) + pr[pl.ds(96, 32), columns].astype(F32)

    for_query, for_head = pl.ds(0, 1024), pl.ds(1024, 256)
    to_query = dot(hidden, wq[...])
    ps[:, for_query] = to_query.astype(BF16)
    share(for_query, 5)
    to_head = dot(hidden, wo[...])
    ps[:, for_head] = to_head.astype(BF16)
    share(for_head, 1)
    queries = (to_query[0:32, :] + others(for_query, 5)).astype(BF16)
    scores = lax.dot_general(queries, gb[...], (((1,), (1,)), ((), ())), preferred_element_type=F32)
    gates = jnp.where(plb[...].astype(F32) > 0.5, jax.nn.sigmoid(scores * (1.0 / 32.0)), 0.0).astype(BF16)
    context = (dot(gates, gb[...]) / counts).astype(BF16)
    embedding = rms_rows((to_head[0:32, :] + others(for_head, 1)) + dot(context, wc[...])).astype(BF16)
    emb_out[...] = embedding

    slots = dot_first(obt[...], embedding)
    ob[:, 0, :] = slots[0:128, :]
    ob[:, 1, :] = slots[128:256, :]

    for i in range(1, 128):
        dp_to, x_to = partner(i, 1)
        remote(ob.at[dp_to * 4 + x_to], eb.at[me], 6, (dp_to, x_to)).start()
    own_slots = pltpu.make_async_copy(ob.at[me], eb.at[me], recv_sem.at[6])
    own_slots.start()
    landed(eb, recv_sem.at[6])

    keep.wait()
    landed(rq.at[pl.ds(0, 127)], send_sem.at[0])
    landed(ns.at[pl.ds(0, 96), :], send_sem.at[2])
    landed(sb.at[pl.ds(16, 2032), :], send_sem.at[3])
    landed(na.at[pl.ds(0, 96), :], send_sem.at[4])
    landed(ps.at[pl.ds(32, 96), for_query], send_sem.at[5])
    landed(ps.at[pl.ds(32, 96), for_head], send_sem.at[1])
    landed(ob.at[pl.ds(0, 127)], send_sem.at[6])
    landed(rl.at[pl.ds(0, 127)], send_sem.at[7])


def finish(emb_in, arrived, centres, emb_out, res_out):
    emb_out[...] = emb_in[...]
    res_out[...] = arrived[...] - centres[...]


def local(
    features_table, self_features, neighbour_ids, neighbour_counts, node_owner, node_row, list_ids, list_owner,
    list_row, centroids, w_self, w_neigh, w_query, w_out, w_context,
):
    vmem, anyw = (pl.BlockSpec(memory_space=m) for m in (pltpu.VMEM, pl.ANY))
    i32 = jnp.int32
    scratch = [
        ((2048, 128), i32), ((2048, 128), i32), ((8192, 128), i32), ((8192, 128), i32), ((2048, 1024), BF16),
        ((8192, 256), BF16), ((1024, 512), BF16), ((1024, 512), BF16), ((512, 1024), BF16), ((512, 256), BF16),
        ((1024, 256), BF16),
        ((2048, 256), BF16), ((128, 1, 128), F32), ((128, 1, 128), F32), ((128, 1, 128), F32), ((128, 1, 128), F32), ((128, 128), BF16), ((32, 128), i32), ((32, 128), i32),
        ((2048, 1024), BF16), ((2048, 1024), BF16), ((32, 2048), BF16), ((32, 256), BF16), ((128, 1024), BF16),
        ((128, 1024), BF16), ((128, 512), F32), ((128, 1280), BF16), ((128, 1280), BF16), ((128, 2, 256), F32), ((128, 2, 256), F32),
    ]
    embedding, arrived, centres = pl.pallas_call(
        kernel,
        out_shape=(jax.ShapeDtypeStruct((32, 256), BF16),) + (jax.ShapeDtypeStruct((128, 2, 256), F32),) * 2,
        in_specs=[anyw] * 15,
        out_specs=(vmem, vmem, anyw),
        scratch_shapes=[pltpu.VMEM((32, 32), i32), pltpu.VMEM((1, 32), i32), pltpu.SMEM((32,), i32), pltpu.VMEM((1, 32), i32), pltpu.VMEM((32, 1024), BF16)]
        + [pltpu.VMEM(s, t) for s, t in scratch]
        + [pltpu.SemaphoreType.DMA((n,)) for n in (16, 8, 8, 8, 8)],
        compiler_params=pltpu.CompilerParams(collective_id=0, has_side_effects=True, vmem_limit_bytes=56 << 20),
    )(
        neighbour_ids, neighbour_counts.reshape(1, 32), list_ids.reshape(1, 32), self_features,
        node_owner.reshape(2048, 128), node_row.reshape(2048, 128), list_owner.reshape(8192, 128),
        list_row.reshape(8192, 128), features_table, centroids, w_self, w_neigh, w_query, w_out, w_context,
    )
    return pl.pallas_call(
        finish,
        out_shape=(jax.ShapeDtypeStruct((32, 256), BF16), jax.ShapeDtypeStruct((128, 2, 256), F32)),
        in_specs=[vmem] * 3,
        out_specs=(vmem, vmem),
    )(embedding, arrived, centres)


def solution(mesh):
    placed = (
        P(("dp", "mp"), None),
        P(("dp", "mp"), None),
        P(("dp", "mp"), None),
        P(("dp", "mp")),
        P(),
        P(),
        P(("dp", "mp")),
        P(),
        P(),
        P(("dp", "mp"), None),
        P(None, "mp"),
        P(None, "mp"),
        P("mp", None),
        P("mp", None),
        P(),
    )
    return jax.shard_map(
        local,
        mesh=mesh,
        in_specs=placed,
        out_specs=(P(("dp", "mp"), None), P(("dp", "mp"), None, None)),
        check_vma=False,
    )
```
